32 devices in a mesh: dp: 8 (over y, x, core), tensor: 4 (over z).
Axes of the slice: x: 2, y: 2, z: 4, core: 2. Of those that a mesh axis runs over, the one named last changes fastest.
Arguments:
- layer_input: bfloat16 [8, 512, 1024], P('dp', 'tensor'), may hold values from -6 to 6
- qkv_weight: bfloat16 [1024, 3072], P('dp', 'tensor'), may hold values from -0.1875 to 0.1875
- query_bias: float32 [1024], replicated, may hold values from -3 to 3
- value_bias: float32 [1024], replicated, may hold values from -3 to 3
- out_weight: bfloat16 [1024, 1024], P('tensor', 'dp'), may hold values from -1.5 to 1.5
- out_bias: float32 [1024], replicated, may hold values from -3 to 3
- attn_norm_gain: float32 [1024], replicated, may hold values from 0.5 to 1.5
- attn_norm_bias: float32 [1024], replicated, may hold values from -3 to 3
- ffn_in_weight: bfloat16 [1024, 4096], P('dp', 'tensor'), may hold values from -0.1875 to 0.1875
- ffn_in_bias: float32 [4096], replicated, may hold values from -3 to 3
- ffn_out_weight: bfloat16 [4096, 1024], P('tensor', 'dp'), may hold values from -0.09375 to 0.09375
- ffn_out_bias: float32 [1024], replicated, may hold values from -3 to 3
- ffn_norm_gain: float32 [1024], replicated, may hold values from 0.5 to 1.5
- ffn_norm_bias: float32 [1024], replicated, may hold values from -3 to 3
- grad_output: bfloat16 [8, 512, 1024], P('dp', 'tensor'), may hold values from -6 to 6
Outputs:
- layer_output: bfloat16 [8, 512, 1024], P('dp', 'tensor')
- grad_input: bfloat16 [8, 512, 1024], P('dp', 'tensor')
- grad_qkv_weight: float32 [1024, 3072], P('dp', 'tensor')
- grad_query_bias: float32 [1024], replicated
- grad_value_bias: float32 [1024], replicated
- grad_out_weight: float32 [1024, 1024], P('tensor', 'dp')
- grad_out_bias: float32 [1024], replicated
- grad_attn_norm_gain: float32 [1024], replicated
- grad_attn_norm_bias: float32 [1024], replicated
- grad_ffn_in_weight: float32 [1024, 4096], P('dp', 'tensor')
- grad_ffn_in_bias: float32 [4096], replicated
- grad_ffn_out_weight: float32 [4096, 1024], P('tensor', 'dp')
- grad_ffn_out_bias: float32 [1024], replicated
- grad_ffn_norm_gain: float32 [1024], replicated
- grad_ffn_norm_bias: float32 [1024], replicated
The draws below stay inside these ranges and needn't reach their ends.
All inputs are finite; a program needn't handle non-finite values.
Results may differ from the reference program's by a relative error of at most 0.02.
Values may be sent and summed in bfloat16 or wider, within the bound.
A program may use at most 64 MiB of HBM per device.

```python
import jax
import jax.numpy as jnp
from jax import lax

D = 1024
HEADS = 16
HD = 64
FF = 4096
LENGTH = 512
BATCH = 8


def level_of(key, dims, split, low, top_value):
    level, own = 1.0, jax.random.fold_in(key, 6)
    for axis_at, parts in split:
        heights = jnp.exp(jax.random.uniform(jax.random.fold_in(own, axis_at), (parts,), jnp.float32, low / len(split), top_value / len(split)))
        level = level * jnp.repeat(heights, dims[axis_at] // parts).reshape([-1 if axis == axis_at else 1 for axis in range(len(dims))])
    return level


def centred(own_key, shape, deviation, most, cuts=(), kind=jnp.bfloat16):
    array = jax.random.normal(own_key, shape, jnp.float32) * deviation
    if len(cuts) > 0:
        array = level_of(own_key, shape, cuts, -0.22, 0.18) * array
    return jnp.clip(array, min=-most, max=most).astype(kind)


def setup_inputs(seed: int = 0) -> dict:
    keys = jax.random.split(jax.random.key(seed), 16)
    layer_input = centred(keys[0], (BATCH, LENGTH, D), 1.0, 6.0, ((0, 8), (1, 4)))
    qkv_weight = centred(keys[1], (D, 3 * D), D ** -0.5, 0.1875, ((0, 8), (1, 4)))
    query_bias = centred(keys[2], (D,), 0.5, 3.0, (), jnp.float32)
    value_bias = centred(keys[3], (D,), 0.5, 3.0, (), jnp.float32)
    out_weight = centred(keys[4], (D, D), (D // 64) ** -0.5, 1.5, ((0, 4), (1, 8)))
    out_bias = centred(keys[5], (D,), 0.5, 3.0, (), jnp.float32)
    attn_norm_gain = jnp.clip(1.0 + 0.1 * jax.random.normal(keys[6], (D,), jnp.float32), 0.5, 1.5)
    attn_norm_bias = centred(keys[7], (D,), 0.5, 3.0, (), jnp.float32)
    ffn_in_weight = centred(keys[8], (D, FF), D ** -0.5, 0.1875, ((0, 8), (1, 4)))
    ffn_in_bias = centred(keys[9], (FF,), 0.5, 3.0, (), jnp.float32)
    ffn_out_weight = centred(keys[10], (FF, D), FF ** -0.5, 0.09375, ((0, 4), (1, 8)))
    ffn_out_bias = centred(keys[11], (D,), 0.5, 3.0, (), jnp.float32)
    ffn_norm_gain = jnp.clip(1.0 + 0.1 * jax.random.normal(keys[12], (D,), jnp.float32), 0.5, 1.5)
    ffn_norm_bias = centred(keys[13], (D,), 0.5, 3.0, (), jnp.float32)
    grad_output = centred(keys[14], (BATCH, LENGTH, D), 1.0, 6.0, ((0, 8), (1, 4)))
    return dict(layer_input=layer_input, qkv_weight=qkv_weight, query_bias=query_bias, value_bias=value_bias, out_weight=out_weight, out_bias=out_bias, attn_norm_gain=attn_norm_gain, attn_norm_bias=attn_norm_bias, ffn_in_weight=ffn_in_weight, ffn_in_bias=ffn_in_bias, ffn_out_weight=ffn_out_weight, ffn_out_bias=ffn_out_bias, ffn_norm_gain=ffn_norm_gain, ffn_norm_bias=ffn_norm_bias, grad_output=grad_output)


highest_precision = lax.Precision.HIGHEST
norm_eps = 1e-05
root_half = 0.7071067811865476

@jax.custom_vjp
def low(v):
    return lax.optimization_barrier(v.astype(jnp.bfloat16)).astype(jnp.float32)

@jax.custom_vjp
def low_back(v):
    return v

def low_keep(v):
    return (low(v), None)

def low_pass(kept, grad):
    return (grad,)

def back_keep(v):
    return (v, None)

def back_low(kept, grad):
    return (low(grad),)
low.defvjp(low_keep, low_pass)
low_back.defvjp(back_keep, back_low)

def matmul_high(first_op, second_op):
    return jnp.dot(first_op, second_op, precision=highest_precision, preferred_element_type=jnp.float32)

def layer_norm(residual, norm_gain, offset):
    center = residual - lax.optimization_barrier(jnp.mean(residual, axis=-1, keepdims=True))
    variance = lax.optimization_barrier(jnp.mean(center * center, axis=-1, keepdims=True))
    return center * lax.rsqrt(variance + norm_eps) * norm_gain + offset

def gelu_exact(preact):
    return 0.5 * preact * (1.0 + lax.erf(preact * root_half))

def forward(layer_input, qkv_weight, query_bias, value_bias, out_weight, out_bias, attn_norm_gain, attn_norm_bias, ffn_in_weight, ffn_in_bias, ffn_out_weight, ffn_out_bias, ffn_norm_gain, ffn_norm_bias):
    length = layer_input.shape[0]
    packed = matmul_high(layer_input, qkv_weight).reshape(length, HEADS, 3, HD)
    queries = low(low_back(packed[:, :, 0] + query_bias.reshape(HEADS, HD)))
    key_rows = low(low_back(packed[:, :, 1]))
    values = low(low_back(packed[:, :, 2] + value_bias.reshape(HEADS, HD)))
    scores = low_back(jnp.einsum('qhe,khe->hqk', queries, key_rows, precision=highest_precision) * HD ** (-0.5))
    shifted = jnp.exp(scores - lax.optimization_barrier(jnp.max(scores, axis=-1, keepdims=True)))
    probs = low(shifted / lax.optimization_barrier(jnp.sum(shifted, axis=-1, keepdims=True)))
    attended = jnp.einsum('hqk,khe->qhe', probs, values, precision=highest_precision)
    attended = low(low_back(attended)).reshape(length, HEADS * HD)
    attn_branch = low_back(matmul_high(attended, out_weight) + out_bias)
    normed_one = low(layer_norm(layer_input + attn_branch, attn_norm_gain, attn_norm_bias))
    inner_pre = low_back(matmul_high(normed_one, ffn_in_weight) + ffn_in_bias)
    activated = low(low_back(gelu_exact(inner_pre)))
    ffn_branch = low_back(matmul_high(activated, ffn_out_weight) + ffn_out_bias)
    return layer_norm(normed_one + ffn_branch, ffn_norm_gain, ffn_norm_bias)

def reference(layer_input, qkv_weight, query_bias, value_bias, out_weight, out_bias, attn_norm_gain, attn_norm_bias, ffn_in_weight, ffn_in_bias, ffn_out_weight, ffn_out_bias, ffn_norm_gain, ffn_norm_bias, grad_output):
    params = tuple((member.astype(jnp.float32) for member in (qkv_weight, query_bias, value_bias, out_weight, out_bias, attn_norm_gain, attn_norm_bias, ffn_in_weight, ffn_in_bias, ffn_out_weight, ffn_out_bias, ffn_norm_gain, ffn_norm_bias)))

    def one_sequence(totals, paired):
        inputs, cotangent = paired
        result, pullback = jax.vjp(forward, inputs.astype(jnp.float32), *params)
        gradients = pullback(cotangent.astype(jnp.float32))
        totals = tuple((running + gradient for running, gradient in zip(totals, gradients[1:])))
        return (totals, (result.astype(jnp.bfloat16), gradients[0].astype(jnp.bfloat16)))
    zero_sums = tuple((jnp.zeros(member.shape, jnp.float32) for member in params))
    totals, outputs = lax.scan(one_sequence, zero_sums, (layer_input, grad_output))
    return (outputs[0], outputs[1], totals[0], totals[1], totals[2], totals[3], totals[4], totals[5], totals[6], totals[7], totals[8], totals[9], totals[10], totals[11], totals[12])
```

```python
import jax
import jax.numpy as jnp
from jax import lax
from jax.sharding import PartitionSpec as P

HEADS = 16
HD = 64
FF = 4096


norm_eps = 1e-05
root_half = 0.7071067811865476
inv_root_tau = 0.3989422804014327


def matmul(first_op, second_op):
    return jnp.dot(first_op, second_op, preferred_element_type=jnp.float32)


def matmul_by_transpose(first_op, second_op):
    return lax.dot_general(
        first_op, second_op, (((1,), (1,)), ((), ())), preferred_element_type=jnp.float32
    )


def transpose_matmul(first_op, second_op):
    return lax.dot_general(
        first_op, second_op, (((0,), (0,)), ((), ())), preferred_element_type=jnp.float32
    )


def norm_forward(residual, norm_gain, offset):
    center = residual - jnp.mean(residual, axis=-1, keepdims=True)
    variance = jnp.mean(center * center, axis=-1, keepdims=True)
    inv_std = lax.rsqrt(variance + norm_eps)
    normed = center * inv_std
    return (normed * norm_gain + offset, normed, inv_std)


def norm_backward(upstream, normed, inv_std, norm_gain):
    scaled = upstream * norm_gain
    centered = scaled - jnp.mean(scaled, axis=-1, keepdims=True)
    return inv_std * (centered - normed * jnp.mean(scaled * normed, axis=-1, keepdims=True))


def gelu_exact(preact):
    return 0.5 * preact * (1.0 + lax.erf(preact * root_half))


def gelu_slope(preact):
    return (
        0.5 * (1.0 + lax.erf(preact * root_half))
        + preact * jnp.exp(-0.5 * preact * preact) * inv_root_tau
    )


def attend(operands):
    queries, key_rows, values = operands
    scores = jnp.einsum(
        "qhe,khe->hqk", queries, key_rows, preferred_element_type=jnp.float32
    ) * HD ** (-0.5)
    row_max = jnp.max(scores, axis=-1, keepdims=True)
    shifted = jnp.exp(scores - row_max)
    row_total = jnp.sum(shifted, axis=-1, keepdims=True)
    probs = (shifted / row_total).astype(jnp.bfloat16)
    attended = jnp.einsum("hqk,khe->qhe", probs, values, preferred_element_type=jnp.float32).astype(
        jnp.bfloat16
    )
    return (attended, row_max + jnp.log(row_total))


def attend_back(operands):
    queries, key_rows, values, log_total, grad_attended = operands
    scores = jnp.einsum(
        "qhe,khe->hqk", queries, key_rows, preferred_element_type=jnp.float32
    ) * HD ** (-0.5)
    probs = jnp.exp(scores - log_total)
    grad_probs = jnp.einsum(
        "qhe,khe->hqk", grad_attended, values, preferred_element_type=jnp.float32
    )
    grad_values = jnp.einsum(
        "hqk,qhe->khe",
        probs.astype(jnp.bfloat16),
        grad_attended,
        preferred_element_type=jnp.float32,
    ).astype(jnp.bfloat16)
    row_dot = jnp.sum(probs * grad_probs, axis=-1, keepdims=True)
    grad_scores = (probs * (grad_probs - row_dot)).astype(jnp.bfloat16)
    grad_queries = (
        jnp.einsum("hqk,khe->qhe", grad_scores, key_rows, preferred_element_type=jnp.float32)
        * HD ** (-0.5)
    ).astype(jnp.bfloat16)
    grad_keys = (
        jnp.einsum("hqk,qhe->khe", grad_scores, queries, preferred_element_type=jnp.float32)
        * HD ** (-0.5)
    ).astype(jnp.bfloat16)
    return (grad_queries, grad_keys, grad_values)


def body(
    layer_input,
    qkv_weight,
    query_bias,
    value_bias,
    out_weight,
    out_bias,
    attn_norm_gain,
    attn_norm_bias,
    ffn_in_weight,
    ffn_in_bias,
    ffn_out_weight,
    ffn_out_bias,
    ffn_norm_gain,
    ffn_norm_bias,
    grad_output,
):
    tensor_parts = lax.axis_size("tensor")
    tensor_rank = lax.axis_index("tensor")
    heads_here = HEADS // tensor_parts
    width_here = heads_here * HD
    hidden_here = FF // tensor_parts
    qkv_full, ffn_in_full, out_full, ffn_out_full = (
        lax.all_gather(qkv_weight, "dp", axis=0, tiled=True),
        lax.all_gather(ffn_in_weight, "dp", axis=0, tiled=True),
        lax.all_gather(out_weight, "dp", axis=1, tiled=True),
        lax.all_gather(ffn_out_weight, "dp", axis=1, tiled=True),
    )
    seq_count, piece_len, feature_count = layer_input.shape
    length = piece_len * tensor_parts
    row_count = seq_count * length
    input_full = lax.all_gather(layer_input, "tensor", axis=1, tiled=True)
    input_rows = input_full.reshape(row_count, feature_count)
    packed = matmul(input_rows, qkv_full).reshape(seq_count, length, heads_here, 3, HD)
    query_slice = lax.dynamic_slice_in_dim(
        query_bias.reshape(HEADS, HD), tensor_rank * heads_here, heads_here, 0
    )
    value_slice = lax.dynamic_slice_in_dim(
        value_bias.reshape(HEADS, HD), tensor_rank * heads_here, heads_here, 0
    )
    queries = (packed[:, :, :, 0] + query_slice).astype(jnp.bfloat16)
    key_rows = packed[:, :, :, 1].astype(jnp.bfloat16)
    values = (packed[:, :, :, 2] + value_slice).astype(jnp.bfloat16)
    attended, log_total = lax.map(attend, (queries, key_rows, values))
    attended_rows = attended.reshape(row_count, width_here)
    attn_part = matmul(attended_rows, out_full).reshape(seq_count, length, feature_count)
    attn_branch = (
        lax.psum_scatter(
            attn_part.astype(jnp.bfloat16), "tensor", scatter_dimension=1, tiled=True
        ).astype(jnp.float32)
        + out_bias
    )
    normed_one, unit_one, inv_std_one = norm_forward(
        layer_input.astype(jnp.float32) + attn_branch, attn_norm_gain, attn_norm_bias
    )
    normed_low = normed_one.astype(jnp.bfloat16)
    normed_full = lax.all_gather(normed_low, "tensor", axis=1, tiled=True)
    normed_rows = normed_full.reshape(row_count, feature_count)
    inner_bias = lax.dynamic_slice_in_dim(ffn_in_bias, tensor_rank * hidden_here, hidden_here, 0)
    inner_pre = matmul(normed_rows, ffn_in_full) + inner_bias
    activated = gelu_exact(inner_pre).astype(jnp.bfloat16)
    ffn_part = matmul(activated, ffn_out_full).reshape(seq_count, length, feature_count)
    ffn_branch = (
        lax.psum_scatter(
            ffn_part.astype(jnp.bfloat16), "tensor", scatter_dimension=1, tiled=True
        ).astype(jnp.float32)
        + ffn_out_bias
    )
    output_f32, unit_two, inv_std_two = norm_forward(
        normed_low.astype(jnp.float32) + ffn_branch, ffn_norm_gain, ffn_norm_bias
    )
    layer_output = output_f32.astype(jnp.bfloat16)
    grad_top = grad_output.astype(jnp.float32)
    grad_ffn_norm_gain = jnp.sum(grad_top * unit_two, axis=(0, 1))
    grad_ffn_norm_bias = jnp.sum(grad_top, axis=(0, 1))
    grad_resid_two = norm_backward(grad_top, unit_two, inv_std_two, ffn_norm_gain)
    grad_branch_two = grad_resid_two.astype(jnp.bfloat16)
    grad_ffn_out_bias = jnp.sum(grad_branch_two.astype(jnp.float32), axis=(0, 1))
    branch_two_full = lax.all_gather(grad_branch_two, "tensor", axis=1, tiled=True)
    branch_two_rows = branch_two_full.reshape(row_count, feature_count)
    grad_activated = matmul_by_transpose(branch_two_rows, ffn_out_full).astype(jnp.bfloat16)
    grad_ffn_out_local = transpose_matmul(branch_two_rows, activated)
    grad_inner = (grad_activated.astype(jnp.float32) * gelu_slope(inner_pre)).astype(jnp.bfloat16)
    inner_bias_grad = jnp.sum(grad_inner.astype(jnp.float32), axis=0)
    grad_ffn_in_local = transpose_matmul(normed_rows, grad_inner)
    normed_part = matmul_by_transpose(grad_inner, ffn_in_full).reshape(
        seq_count, length, feature_count
    )
    grad_normed = (
        lax.psum_scatter(
            normed_part.astype(jnp.bfloat16), "tensor", scatter_dimension=1, tiled=True
        ).astype(jnp.float32)
        + grad_resid_two
    )
    grad_attn_norm_gain = jnp.sum(grad_normed * unit_one, axis=(0, 1))
    grad_attn_norm_bias = jnp.sum(grad_normed, axis=(0, 1))
    grad_resid_one = norm_backward(grad_normed, unit_one, inv_std_one, attn_norm_gain)
    grad_branch_one = grad_resid_one.astype(jnp.bfloat16)
    grad_out_bias = jnp.sum(grad_branch_one.astype(jnp.float32), axis=(0, 1))
    branch_one_full = lax.all_gather(grad_branch_one, "tensor", axis=1, tiled=True)
    branch_one_rows = branch_one_full.reshape(row_count, feature_count)
    grad_attended = (
        matmul_by_transpose(branch_one_rows, out_full)
        .astype(jnp.bfloat16)
        .reshape(seq_count, length, heads_here, HD)
    )
    grad_out_local = transpose_matmul(branch_one_rows, attended_rows)
    grad_queries, grad_keys, grad_values = lax.map(
        attend_back, (queries, key_rows, values, log_total, grad_attended)
    )
    grad_packed = jnp.stack((grad_queries, grad_keys, grad_values), axis=3).reshape(
        row_count, 3 * width_here
    )
    grad_qkv_local = transpose_matmul(input_rows, grad_packed)
    input_part = matmul_by_transpose(grad_packed, qkv_full).reshape(
        seq_count, length, feature_count
    )
    grad_input = (
        lax.psum_scatter(
            input_part.astype(jnp.bfloat16), "tensor", scatter_dimension=1, tiled=True
        ).astype(jnp.float32)
        + grad_resid_one
    ).astype(jnp.bfloat16)
    low_kind = jnp.bfloat16
    ffn_grads = lax.psum_scatter(
        jnp.concatenate((grad_ffn_in_local.astype(low_kind), grad_ffn_out_local.astype(low_kind)), axis=1),
        "dp",
        scatter_dimension=0,
        tiled=True,
    ).astype(jnp.float32)
    attn_grads = lax.psum_scatter(
        jnp.concatenate((grad_qkv_local.astype(low_kind), grad_out_local.astype(low_kind)), axis=1),
        "dp",
        scatter_dimension=0,
        tiled=True,
    ).astype(jnp.float32)
    grad_ffn_in_weight = ffn_grads[:, :hidden_here]
    grad_ffn_out_weight = ffn_grads[:, hidden_here:].T
    grad_qkv_weight = attn_grads[:, : 3 * width_here]
    grad_out_weight = attn_grads[:, 3 * width_here :].T
    query_grad_here = jnp.sum(grad_queries.astype(jnp.float32), axis=(0, 1)).reshape(width_here)
    value_grad_here = jnp.sum(grad_values.astype(jnp.float32), axis=(0, 1)).reshape(width_here)
    query_padded = lax.dynamic_update_slice_in_dim(
        jnp.zeros((HEADS * HD,), jnp.float32), query_grad_here, tensor_rank * width_here, 0
    )
    value_padded = lax.dynamic_update_slice_in_dim(
        jnp.zeros((HEADS * HD,), jnp.float32), value_grad_here, tensor_rank * width_here, 0
    )
    inner_padded = lax.dynamic_update_slice_in_dim(
        jnp.zeros((FF,), jnp.float32), inner_bias_grad, tensor_rank * hidden_here, 0
    )
    small = (
        query_padded,
        value_padded,
        grad_out_bias,
        grad_attn_norm_gain,
        grad_attn_norm_bias,
        inner_padded,
        grad_ffn_out_bias,
        grad_ffn_norm_gain,
        grad_ffn_norm_bias,
    )
    flat = lax.psum(jnp.concatenate(small).reshape(-1, 128), ("dp", "tensor")).reshape(-1)
    summed, at = [], 0
    for member in small:
        summed.append(flat[at : at + member.shape[0]])
        at += member.shape[0]
    return (
        layer_output,
        grad_input,
        grad_qkv_weight,
        summed[0],
        summed[1],
        grad_out_weight,
        summed[2],
        summed[3],
        summed[4],
        grad_ffn_in_weight,
        summed[5],
        grad_ffn_out_weight,
        summed[6],
        summed[7],
        summed[8],
    )


def solution(mesh):
    placed = (
        P("dp", "tensor", None),
        P("dp", "tensor"),
        P(),
        P(),
        P("tensor", "dp"),
        P(),
        P(),
        P(),
        P("dp", "tensor"),
        P(),
        P("tensor", "dp"),
        P(),
        P(),
        P(),
        P("dp", "tensor", None),
    )
    return jax.shard_map(
        body,
        mesh=mesh,
        in_specs=placed,
        out_specs=(
            P("dp", "tensor", None),
            P("dp", "tensor", None),
            P("dp", "tensor"),
            P(),
            P(),
            P("tensor", "dp"),
            P(),
            P(),
            P(),
            P("dp", "tensor"),
            P(),
            P("tensor", "dp"),
            P(),
            P(),
            P(),
        ),
        check_vma=False,
    )
```

```python
import functools

import jax
import jax.numpy as jnp
from jax import lax
from jax.experimental import pallas as pl
from jax.experimental.pallas import tpu as pltpu
from jax.sharding import PartitionSpec as P

HEADS = 16
HD = 64
FF = 4096


norm_eps = 1e-05
root_half = 0.7071067811865476
inv_root_tau = 0.3989422804014327


def matmul(first_op, second_op):
    return jnp.dot(first_op, second_op, preferred_element_type=jnp.float32)


def matmul_by_transpose(first_op, second_op):
    return lax.dot_general(
        first_op, second_op, (((1,), (1,)), ((), ())), preferred_element_type=jnp.float32
    )


def transpose_matmul(first_op, second_op):
    return lax.dot_general(
        first_op, second_op, (((0,), (0,)), ((), ())), preferred_element_type=jnp.float32
    )


def norm_forward(residual, norm_gain, offset):
    center = residual - jnp.mean(residual, axis=-1, keepdims=True)
    variance = jnp.mean(center * center, axis=-1, keepdims=True)
    inv_std = lax.rsqrt(variance + norm_eps)
    normed = center * inv_std
    return (normed * norm_gain + offset, normed, inv_std)


def norm_backward(upstream, normed, inv_std, norm_gain):
    scaled = upstream * norm_gain
    centered = scaled - jnp.mean(scaled, axis=-1, keepdims=True)
    return inv_std * (centered - normed * jnp.mean(scaled * normed, axis=-1, keepdims=True))


def gelu_exact(preact):
    return 0.5 * preact * (1.0 + lax.erf(preact * root_half))


def gelu_slope(preact):
    return (
        0.5 * (1.0 + lax.erf(preact * root_half))
        + preact * jnp.exp(-0.5 * preact * preact) * inv_root_tau
    )


MESH = pl.DeviceIdType.MESH
in_vmem = pl.BlockSpec(memory_space=pltpu.VMEM)
row_chunks = 4


def line_barrier(z, n):
    barrier = pltpu.get_barrier_semaphore()
    for there, other in ((z > 0, z - 1), (z < n - 1, z + 1)):

        @pl.when(there)
        def _():
            pl.semaphore_signal(barrier, inc=1, device_id={"tensor": other}, device_id_type=MESH)

    inner = (z > 0) & (z < n - 1)

    @pl.when(inner)
    def _():
        pl.semaphore_wait(barrier, 2)

    @pl.when(jnp.logical_not(inner))
    def _():
        pl.semaphore_wait(barrier, 1)


class LineSum:
    def __init__(self, z, n, part, stage, from_left, from_right, acc, send, recv):
        self.z, self.n = z, n
        self.part, self.stage, self.acc = part, stage, acc
        self.bufs, self.send, self.recv = (from_left, from_right), send, recv
        self.rows = part.shape[1] // row_chunks

    def at(self, c):
        return pl.ds(c * self.rows, self.rows)

    def copy(self, way, d, c, src):
        z, n = self.z, self.n
        other = lax.rem(z + 1, n) if way == 0 else lax.rem(z + n - 1, n)
        return pltpu.make_async_remote_copy(
            src_ref=src.at[d, self.at(c)],
            dst_ref=self.bufs[way].at[d, self.at(c)],
            send_sem=self.send.at[way, d, c],
            recv_sem=self.recv.at[way, d, c],
            device_id={"tensor": other},
            device_id_type=MESH,
        )

    def pairs(self):
        for k in range(self.n - 1):
            yield 0, self.n - 1 - k, self.z < self.n - 1 - k
            yield 1, k, self.z > k

    def start_ends(self):
        for c in range(row_chunks):
            for way, d, active in self.pairs():

                @pl.when(self.z == (0 if way == 0 else self.n - 1))
                def _():
                    self.copy(way, d, c, self.part).start()

    def forward(self, c):
        for way, d, active in self.pairs():
            inner = self.z > 0 if way == 0 else self.z < self.n - 1

            @pl.when(active & inner)
            def _():
                self.copy(way, d, c, self.part).wait_recv()
                at = self.at(c)
                total = self.part[d, at].astype(jnp.float32) + self.bufs[way][d, at].astype(jnp.float32)
                self.stage[d, at] = total.astype(jnp.bfloat16)
                self.copy(way, d, c, self.stage).start()

    def finish(self, c):
        z, at = self.z, self.at(c)
        self.acc[at] = self.part[z, at].astype(jnp.float32)
        for way, there in ((0, z > 0), (1, z < self.n - 1)):

            @pl.when(there)
            def _():
                self.copy(way, z, c, self.part).wait_recv()
                self.acc[at] += self.bufs[way][z, at].astype(jnp.float32)

        return self.acc[at]

    def drain(self):
        for c in range(row_chunks):
            for way, d, active in self.pairs():

                @pl.when(active)
                def _():
                    self.copy(way, d, c, self.part).wait_send()


class LineGather:
    def __init__(self, z, n, full, send, recv):
        self.z, self.n, self.full, self.send, self.recv = z, n, full, send, recv
        self.rows = full.shape[1] // row_chunks

    def copy(self, way, s, c):
        z, n = self.z, self.n
        other = lax.rem(z + 1, n) if way == 0 else lax.rem(z + n - 1, n)
        block = self.full.at[s, pl.ds(c * self.rows, self.rows)]
        return pltpu.make_async_remote_copy(
            src_ref=block,
            dst_ref=block,
            send_sem=self.send.at[way, s, c],
            recv_sem=self.recv.at[s, c],
            device_id={"tensor": other},
            device_id_type=MESH,
        )

    def start(self, c):
        for way, there in ((0, self.z < self.n - 1), (1, self.z > 0)):

            @pl.when(there)
            def _():
                self.copy(way, self.z, c).start()

    def forward(self, c):
        for k in range(1, self.n):
            for way, s, there, onward in (
                (0, self.z - k, self.z >= k, self.z < self.n - 1),
                (1, self.z + k, self.z < self.n - k, self.z > 0),
            ):

                @pl.when(there)
                def _():
                    self.copy(way, s, c).wait_recv()

                    @pl.when(onward)
                    def _():
                        self.copy(way, s, c).start()

    def drain(self):
        for c in range(row_chunks):
            for s in range(self.n):
                for way, sent in (
                    (0, (self.z >= s) & (self.z < self.n - 1)),
                    (1, (self.z <= s) & (self.z > 0)),
                ):

                    @pl.when(sent)
                    def _():
                        self.copy(way, s, c).wait_send()


def turn_kernel(n, middle, side_count, out_count, *refs):
    part, side = refs[0], refs[1 : 1 + side_count]
    full, outs = refs[1 + side_count], refs[2 + side_count : 2 + side_count + out_count]
    stage, from_left, from_right, acc, sum_send, sum_recv, send, recv = refs[2 + side_count + out_count :]
    z = lax.axis_index("tensor")
    line_barrier(z, n)
    summing = LineSum(z, n, part, stage, from_left, from_right, acc, sum_send, sum_recv)
    gather = LineGather(z, n, full, send, recv)
    summing.start_ends()
    summing.forward(0)
    for c in range(row_chunks):
        if c + 1 < row_chunks:
            summing.forward(c + 1)
        total = summing.finish(c)
        full[z, summing.at(c)] = middle(c, summing.at(c), total, side, outs)
        gather.start(c)
        if c > 0:
            gather.forward(c - 1)
    gather.forward(row_chunks - 1)
    summing.drain()
    gather.drain()


def turn(n, number, name, middle, part, side, out_shapes):
    shape = part.shape
    return pl.pallas_call(
        functools.partial(turn_kernel, n, middle, len(side), len(out_shapes)),
        out_shape=[jax.ShapeDtypeStruct(shape, jnp.bfloat16)] + out_shapes,
        in_specs=[in_vmem] * (1 + len(side)),
        out_specs=[in_vmem] * (1 + len(out_shapes)),
        scratch_shapes=[pltpu.VMEM(shape, jnp.bfloat16)] * 3
        + [
            pltpu.VMEM(shape[1:], jnp.float32),
            pltpu.SemaphoreType.DMA((2, n, row_chunks)),
            pltpu.SemaphoreType.DMA((2, n, row_chunks)),
            pltpu.SemaphoreType.DMA((2, n, row_chunks)),
            pltpu.SemaphoreType.DMA((n, row_chunks)),
        ],
        compiler_params=pltpu.CompilerParams(
            collective_id=number, has_side_effects=True, vmem_limit_bytes=32 * 1024 * 1024
        ),
        cost_estimate=pl.CostEstimate(flops=60000000, bytes_accessed=40000000, transcendentals=0),
        name=name,
    )(part, *side)


def add_small(ref, c, values):
    for i, value in enumerate(values):
        row = jnp.sum(value, axis=0, keepdims=True)
        ref[i : i + 1] = row if c == 0 else ref[i : i + 1] + row


def middle_one(c, at, total, side, outs):
    layer_input, out_bias, gain, offset = side
    unit_out, inv_out, low_out = outs
    normed, unit, inv_std = norm_forward(
        layer_input[at].astype(jnp.float32) + (total + out_bias[...]), gain[...], offset[...]
    )
    low_value = normed.astype(jnp.bfloat16)
    unit_out[at] = unit
    inv_out[at] = jnp.broadcast_to(inv_std, (inv_std.shape[0], 128))
    low_out[at] = low_value
    return low_value


def middle_two(c, at, total, side, outs):
    low_in, bias, gain, offset, upstream = side
    output, resid_out, small = outs
    result, unit, inv_std = norm_forward(
        low_in[at].astype(jnp.float32) + (total + bias[...]), gain[...], offset[...]
    )
    output[at] = result.astype(jnp.bfloat16)
    grad_top = upstream[at].astype(jnp.float32)
    resid = norm_backward(grad_top, unit, inv_std, gain[...])
    resid_out[at] = resid
    branch = resid.astype(jnp.bfloat16)
    add_small(small, c, (grad_top * unit, grad_top, branch.astype(jnp.float32)))
    return branch


def middle_three(c, at, total, side, outs):
    resid_two, unit_one, inv_one, gain = side
    resid_out, small = outs
    grad_normed = total + resid_two[at]
    unit = unit_one[at]
    resid = norm_backward(grad_normed, unit, inv_one[at, 0:1], gain[...])
    resid_out[at] = resid
    branch = resid.astype(jnp.bfloat16)
    add_small(small, c, (grad_normed * unit, grad_normed, branch.astype(jnp.float32)))
    return branch


def attend(operands):
    queries, key_rows, values = operands
    scores = jnp.einsum(
        "qhe,khe->hqk", queries, key_rows, preferred_element_type=jnp.float32
    ) * HD ** (-0.5)
    row_max = jnp.max(scores, axis=-1, keepdims=True)
    shifted = jnp.exp(scores - row_max)
    row_total = jnp.sum(shifted, axis=-1, keepdims=True)
    probs = (shifted / row_total).astype(jnp.bfloat16)
    attended = jnp.einsum("hqk,khe->qhe", probs, values, preferred_element_type=jnp.float32).astype(
        jnp.bfloat16
    )
    return (attended, row_max + jnp.log(row_total))


def attend_back(operands):
    queries, key_rows, values, log_total, grad_attended = operands
    scores = jnp.einsum(
        "qhe,khe->hqk", queries, key_rows, preferred_element_type=jnp.float32
    ) * HD ** (-0.5)
    probs = jnp.exp(scores - log_total)
    grad_probs = jnp.einsum(
        "qhe,khe->hqk", grad_attended, values, preferred_element_type=jnp.float32
    )
    grad_values = jnp.einsum(
        "hqk,qhe->khe",
        probs.astype(jnp.bfloat16),
        grad_attended,
        preferred_element_type=jnp.float32,
    ).astype(jnp.bfloat16)
    row_dot = jnp.sum(probs * grad_probs, axis=-1, keepdims=True)
    grad_scores = (probs * (grad_probs - row_dot)).astype(jnp.bfloat16)
    grad_queries = (
        jnp.einsum("hqk,khe->qhe", grad_scores, key_rows, preferred_element_type=jnp.float32)
        * HD ** (-0.5)
    ).astype(jnp.bfloat16)
    grad_keys = (
        jnp.einsum("hqk,qhe->khe", grad_scores, queries, preferred_element_type=jnp.float32)
        * HD ** (-0.5)
    ).astype(jnp.bfloat16)
    return (grad_queries, grad_keys, grad_values)


def body(
    layer_input,
    qkv_weight,
    query_bias,
    value_bias,
    out_weight,
    out_bias,
    attn_norm_gain,
    attn_norm_bias,
    ffn_in_weight,
    ffn_in_bias,
    ffn_out_weight,
    ffn_out_bias,
    ffn_norm_gain,
    ffn_norm_bias,
    grad_output,
):
    tensor_parts = lax.axis_size("tensor")
    tensor_rank = lax.axis_index("tensor")
    heads_here = HEADS // tensor_parts
    width_here = heads_here * HD
    hidden_here = FF // tensor_parts
    qkv_full, ffn_in_full, out_full, ffn_out_full = (
        lax.all_gather(qkv_weight, "dp", axis=0, tiled=True),
        lax.all_gather(ffn_in_weight, "dp", axis=0, tiled=True),
        lax.all_gather(out_weight, "dp", axis=1, tiled=True),
        lax.all_gather(ffn_out_weight, "dp", axis=1, tiled=True),
    )
    seq_count, piece_len, feature_count = layer_input.shape
    length = piece_len * tensor_parts
    row_count = seq_count * length
    input_full = lax.all_gather(layer_input, "tensor", axis=1, tiled=True)
    input_rows = input_full.reshape(row_count, feature_count)
    packed = matmul(input_rows, qkv_full).reshape(seq_count, length, heads_here, 3, HD)
    query_slice = lax.dynamic_slice_in_dim(
        query_bias.reshape(HEADS, HD), tensor_rank * heads_here, heads_here, 0
    )
    value_slice = lax.dynamic_slice_in_dim(
        value_bias.reshape(HEADS, HD), tensor_rank * heads_here, heads_here, 0
    )
    queries = (packed[:, :, :, 0] + query_slice).astype(jnp.bfloat16)
    key_rows = packed[:, :, :, 1].astype(jnp.bfloat16)
    values = (packed[:, :, :, 2] + value_slice).astype(jnp.bfloat16)
    attended, log_total = lax.map(attend, (queries, key_rows, values))
    attended_rows = attended.reshape(row_count, width_here)
    local_rows = seq_count * piece_len

    def by_piece(rows):
        rows = rows.astype(jnp.bfloat16).reshape(seq_count, tensor_parts, piece_len, feature_count)
        return rows.swapaxes(0, 1).reshape(tensor_parts, local_rows, feature_count)

    def by_row(pieces):
        pieces = pieces.reshape(tensor_parts, seq_count, piece_len, feature_count)
        return pieces.swapaxes(0, 1).reshape(row_count, feature_count)

    wide = jax.ShapeDtypeStruct((local_rows, feature_count), jnp.float32)
    low = jax.ShapeDtypeStruct((local_rows, feature_count), jnp.bfloat16)
    sums = jax.ShapeDtypeStruct((3, feature_count), jnp.float32)
    local_input = layer_input.reshape(local_rows, feature_count)
    normed_pieces, unit_one, inv_std_one, normed_low = turn(
        tensor_parts,
        1,
        "turn_one",
        middle_one,
        by_piece(matmul(attended_rows, out_full)),
        (local_input, out_bias[None], attn_norm_gain[None], attn_norm_bias[None]),
        [wide, jax.ShapeDtypeStruct((local_rows, 128), jnp.float32), low],
    )
    normed_rows = by_row(normed_pieces)
    inner_bias = lax.dynamic_slice_in_dim(ffn_in_bias, tensor_rank * hidden_here, hidden_here, 0)
    inner_pre = matmul(normed_rows, ffn_in_full) + inner_bias
    activated = gelu_exact(inner_pre).astype(jnp.bfloat16)
    branch_two_pieces, layer_output, grad_resid_two, small_two = turn(
        tensor_parts,
        2,
        "turn_two",
        middle_two,
        by_piece(matmul(activated, ffn_out_full)),
        (
            normed_low,
            ffn_out_bias[None],
            ffn_norm_gain[None],
            ffn_norm_bias[None],
            grad_output.reshape(local_rows, feature_count),
        ),
        [low, wide, sums],
    )
    layer_output = layer_output.reshape(layer_input.shape)
    grad_ffn_norm_gain, grad_ffn_norm_bias, grad_ffn_out_bias = small_two
    branch_two_rows = by_row(branch_two_pieces)
    grad_activated = matmul_by_transpose(branch_two_rows, ffn_out_full).astype(jnp.bfloat16)
    grad_ffn_out_local = transpose_matmul(branch_two_rows, activated)
    grad_inner = (grad_activated.astype(jnp.float32) * gelu_slope(inner_pre)).astype(jnp.bfloat16)
    inner_bias_grad = jnp.sum(grad_inner.astype(jnp.float32), axis=0)
    grad_ffn_in_local = transpose_matmul(normed_rows, grad_inner)
    branch_one_pieces, grad_resid_one, small_one = turn(
        tensor_parts,
        3,
        "turn_three",
        middle_three,
        by_piece(matmul_by_transpose(grad_inner, ffn_in_full)),
        (grad_resid_two, unit_one, inv_std_one, attn_norm_gain[None]),
        [wide, sums],
    )
    grad_resid_one = grad_resid_one.reshape(layer_input.shape)
    grad_attn_norm_gain, grad_attn_norm_bias, grad_out_bias = small_one
    branch_one_rows = by_row(branch_one_pieces)
    grad_attended = (
        matmul_by_transpose(branch_one_rows, out_full)
        .astype(jnp.bfloat16)
        .reshape(seq_count, length, heads_here, HD)
    )
    grad_out_local = transpose_matmul(branch_one_rows, attended_rows)
    grad_queries, grad_keys, grad_values = lax.map(
        attend_back, (queries, key_rows, values, log_total, grad_attended)
    )
    grad_packed = jnp.stack((grad_queries, grad_keys, grad_values), axis=3).reshape(
        row_count, 3 * width_here
    )
    grad_qkv_local = transpose_matmul(input_rows, grad_packed)
    input_part = matmul_by_transpose(grad_packed, qkv_full).reshape(
        seq_count, length, feature_count
    )
    grad_input = (
        lax.psum_scatter(
            input_part.astype(jnp.bfloat16), "tensor", scatter_dimension=1, tiled=True
        ).astype(jnp.float32)
        + grad_resid_one
    ).astype(jnp.bfloat16)
    low_kind = jnp.bfloat16
    ffn_grads = lax.psum_scatter(
        jnp.concatenate((grad_ffn_in_local.astype(low_kind), grad_ffn_out_local.astype(low_kind)), axis=1),
        "dp",
        scatter_dimension=0,
        tiled=True,
    ).astype(jnp.float32)
    attn_grads = lax.psum_scatter(
        jnp.concatenate((grad_qkv_local.astype(low_kind), grad_out_local.astype(low_kind)), axis=1),
        "dp",
        scatter_dimension=0,
        tiled=True,
    ).astype(jnp.float32)
    grad_ffn_in_weight = ffn_grads[:, :hidden_here]
    grad_ffn_out_weight = ffn_grads[:, hidden_here:].T
    grad_qkv_weight = attn_grads[:, : 3 * width_here]
    grad_out_weight = attn_grads[:, 3 * width_here :].T
    query_grad_here = jnp.sum(grad_queries.astype(jnp.float32), axis=(0, 1)).reshape(width_here)
    value_grad_here = jnp.sum(grad_values.astype(jnp.float32), axis=(0, 1)).reshape(width_here)
    query_padded = lax.dynamic_update_slice_in_dim(
        jnp.zeros((HEADS * HD,), jnp.float32), query_grad_here, tensor_rank * width_here, 0
    )
    value_padded = lax.dynamic_update_slice_in_dim(
        jnp.zeros((HEADS * HD,), jnp.float32), value_grad_here, tensor_rank * width_here, 0
    )
    inner_padded = lax.dynamic_update_slice_in_dim(
        jnp.zeros((FF,), jnp.float32), inner_bias_grad, tensor_rank * hidden_here, 0
    )
    small = (
        query_padded,
        value_padded,
        grad_out_bias,
        grad_attn_norm_gain,
        grad_attn_norm_bias,
        inner_padded,
        grad_ffn_out_bias,
        grad_ffn_norm_gain,
        grad_ffn_norm_bias,
    )
    flat = lax.psum(jnp.concatenate(small).reshape(-1, 128), ("dp", "tensor")).reshape(-1)
    summed, at = [], 0
    for member in small:
        summed.append(flat[at : at + member.shape[0]])
        at += member.shape[0]
    return (
        layer_output,
        grad_input,
        grad_qkv_weight,
        summed[0],
        summed[1],
        grad_out_weight,
        summed[2],
        summed[3],
        summed[4],
        grad_ffn_in_weight,
        summed[5],
        grad_ffn_out_weight,
        summed[6],
        summed[7],
        summed[8],
    )


def solution(mesh):
    placed = (
        P("dp", "tensor", None),
        P("dp", "tensor"),
        P(),
        P(),
        P("tensor", "dp"),
        P(),
        P(),
        P(),
        P("dp", "tensor"),
        P(),
        P("tensor", "dp"),
        P(),
        P(),
        P(),
        P("dp", "tensor", None),
    )
    return jax.shard_map(
        body,
        mesh=mesh,
        in_specs=placed,
        out_specs=(
            P("dp", "tensor", None),
            P("dp", "tensor", None),
            P("dp", "tensor"),
            P(),
            P(),
            P("tensor", "dp"),
            P(),
            P(),
            P(),
            P("dp", "tensor"),
            P(),
            P("tensor", "dp"),
            P(),
            P(),
            P(),
        ),
        check_vma=False,
    )
```

```python
import functools

import jax
import jax.numpy as jnp
from jax import lax
from jax.experimental import pallas as pl
from jax.experimental.pallas import tpu as pltpu
from jax.sharding import PartitionSpec as P

HEADS = 16
HD = 64
FF = 4096


norm_eps = 1e-05
root_half = 0.7071067811865476
inv_root_tau = 0.3989422804014327


def matmul(first_op, second_op):
    return jnp.dot(first_op, second_op, preferred_element_type=jnp.float32)


def matmul_by_transpose(first_op, second_op):
    return lax.dot_general(
        first_op, second_op, (((1,), (1,)), ((), ())), preferred_element_type=jnp.float32
    )


def transpose_matmul(first_op, second_op):
    return lax.dot_general(
        first_op, second_op, (((0,), (0,)), ((), ())), preferred_element_type=jnp.float32
    )


def norm_forward(residual, norm_gain, offset):
    center = residual - jnp.mean(residual, axis=-1, keepdims=True)
    variance = jnp.mean(center * center, axis=-1, keepdims=True)
    inv_std = lax.rsqrt(variance + norm_eps)
    normed = center * inv_std
    return (normed * norm_gain + offset, normed, inv_std)


def norm_backward(upstream, normed, inv_std, norm_gain):
    scaled = upstream * norm_gain
    centered = scaled - jnp.mean(scaled, axis=-1, keepdims=True)
    return inv_std * (centered - normed * jnp.mean(scaled * normed, axis=-1, keepdims=True))


def gelu_exact(preact):
    return 0.5 * preact * (1.0 + lax.erf(preact * root_half))


def gelu_slope(preact):
    return (
        0.5 * (1.0 + lax.erf(preact * root_half))
        + preact * jnp.exp(-0.5 * preact * preact) * inv_root_tau
    )


MESH = pl.DeviceIdType.MESH
in_vmem = pl.BlockSpec(memory_space=pltpu.VMEM)
row_chunks = 4


def line_barrier(z, n):
    barrier = pltpu.get_barrier_semaphore()
    for there, other in ((z > 0, z - 1), (z < n - 1, z + 1)):

        @pl.when(there)
        def _():
            pl.semaphore_signal(barrier, inc=1, device_id={"tensor": other}, device_id_type=MESH)

    inner = (z > 0) & (z < n - 1)

    @pl.when(inner)
    def _():
        pl.semaphore_wait(barrier, 2)

    @pl.when(jnp.logical_not(inner))
    def _():
        pl.semaphore_wait(barrier, 1)


class LineSum:
    def __init__(self, z, n, part, stage, from_left, from_right, acc, send, recv):
        self.z, self.n = z, n
        self.part, self.stage, self.acc = part, stage, acc
        self.bufs, self.send, self.recv = (from_left, from_right), send, recv
        self.rows = part.shape[1] // row_chunks

    def at(self, c):
        return pl.ds(c * self.rows, self.rows)

    def copy(self, way, d, c, src):
        z, n = self.z, self.n
        other = lax.rem(z + 1, n) if way == 0 else lax.rem(z + n - 1, n)
        return pltpu.make_async_remote_copy(
            src_ref=src.at[d, self.at(c)],
            dst_ref=self.bufs[way].at[d, self.at(c)],
            send_sem=self.send.at[way, d, c],
            recv_sem=self.recv.at[way, d, c],
            device_id={"tensor": other},
            device_id_type=MESH,
        )

    def pairs(self):
        for k in range(self.n - 1):
            yield 0, self.n - 1 - k, self.z < self.n - 1 - k
            yield 1, k, self.z > k

    def start_ends(self):
        for c in range(row_chunks):
            for way, d, active in self.pairs():

                @pl.when(self.z == (0 if way == 0 else self.n - 1))
                def _():
                    self.copy(way, d, c, self.part).start()

    def forward(self, c):
        for way, d, active in self.pairs():
            inner = self.z > 0 if way == 0 else self.z < self.n - 1

            @pl.when(active & inner)
            def _():
                self.copy(way, d, c, self.part).wait_recv()
                at = self.at(c)
                total = self.part[d, at].astype(jnp.float32) + self.bufs[way][d, at].astype(jnp.float32)
                self.stage[d, at] = total.astype(jnp.bfloat16)
                self.copy(way, d, c, self.stage).start()

    def finish(self, c):
        z, at = self.z, self.at(c)
        self.acc[at] = self.part[z, at].astype(jnp.float32)
        for way, there in ((0, z > 0), (1, z < self.n - 1)):

            @pl.when(there)
            def _():
                self.copy(way, z, c, self.part).wait_recv()
                self.acc[at] += self.bufs[way][z, at].astype(jnp.float32)

        return self.acc[at]

    def drain(self):
        for c in range(row_chunks):
            for way, d, active in self.pairs():

                @pl.when(active)
                def _():
                    self.copy(way, d, c, self.part).wait_send()


class LineGather:
    def __init__(self, z, n, full, send, recv):
        self.z, self.n, self.full, self.send, self.recv = z, n, full, send, recv
        self.rows = full.shape[1] // row_chunks

    def copy(self, way, s, c):
        z, n = self.z, self.n
        other = lax.rem(z + 1, n) if way == 0 else lax.rem(z + n - 1, n)
        block = self.full.at[s, pl.ds(c * self.rows, self.rows)]
        return pltpu.make_async_remote_copy(
            src_ref=block,
            dst_ref=block,
            send_sem=self.send.at[way, s, c],
            recv_sem=self.recv.at[s, c],
            device_id={"tensor": other},
            device_id_type=MESH,
        )

    def start(self, c):
        for way, there in ((0, self.z < self.n - 1), (1, self.z > 0)):

            @pl.when(there)
            def _():
                self.copy(way, self.z, c).start()

    def forward(self, c):
        for k in range(1, self.n):
            for way, s, there, onward in (
                (0, self.z - k, self.z >= k, self.z < self.n - 1),
                (1, self.z + k, self.z < self.n - k, self.z > 0),
            ):

                @pl.when(there)
                def _():
                    self.copy(way, s, c).wait_recv()

                    @pl.when(onward)
                    def _():
                        self.copy(way, s, c).start()

    def drain(self):
        for c in range(row_chunks):
            for s in range(self.n):
                for way, sent in (
                    (0, (self.z >= s) & (self.z < self.n - 1)),
                    (1, (self.z <= s) & (self.z > 0)),
                ):

                    @pl.when(sent)
                    def _():
                        self.copy(way, s, c).wait_send()


def turn_kernel(n, middle, side_count, out_count, *refs):
    part, side = refs[0], refs[1 : 1 + side_count]
    full, outs = refs[1 + side_count], refs[2 + side_count : 2 + side_count + out_count]
    stage, from_left, from_right, acc, sum_send, sum_recv, send, recv = refs[2 + side_count + out_count :]
    z = lax.axis_index("tensor")
    line_barrier(z, n)
    summing = LineSum(z, n, part, stage, from_left, from_right, acc, sum_send, sum_recv)
    gather = LineGather(z, n, full, send, recv)
    summing.start_ends()
    summing.forward(0)
    for c in range(row_chunks):
        if c + 1 < row_chunks:
            summing.forward(c + 1)
        total = summing.finish(c)
        full[z, summing.at(c)] = middle(c, summing.at(c), total, side, outs)
        gather.start(c)
        if c > 0:
            gather.forward(c - 1)
    gather.forward(row_chunks - 1)
    summing.drain()
    gather.drain()


def turn(n, number, name, middle, part, side, out_shapes):
    shape = part.shape
    return pl.pallas_call(
        functools.partial(turn_kernel, n, middle, len(side), len(out_shapes)),
        out_shape=[jax.ShapeDtypeStruct(shape, jnp.bfloat16)] + out_shapes,
        in_specs=[in_vmem] * (1 + len(side)),
        out_specs=[in_vmem] * (1 + len(out_shapes)),
        scratch_shapes=[pltpu.VMEM(shape, jnp.bfloat16)] * 3
        + [
            pltpu.VMEM(shape[1:], jnp.float32),
            pltpu.SemaphoreType.DMA((2, n, row_chunks)),
            pltpu.SemaphoreType.DMA((2, n, row_chunks)),
            pltpu.SemaphoreType.DMA((2, n, row_chunks)),
            pltpu.SemaphoreType.DMA((n, row_chunks)),
        ],
        compiler_params=pltpu.CompilerParams(
            collective_id=number, has_side_effects=True, vmem_limit_bytes=32 * 1024 * 1024
        ),
        cost_estimate=pl.CostEstimate(flops=60000000, bytes_accessed=40000000, transcendentals=0),
        name=name,
    )(part, *side)


def add_small(ref, c, values):
    for i, value in enumerate(values):
        row = jnp.sum(value, axis=0, keepdims=True)
        ref[i : i + 1] = row if c == 0 else ref[i : i + 1] + row


def middle_one(c, at, total, side, outs):
    layer_input, out_bias, gain, offset = side
    unit_out, inv_out, low_out = outs
    normed, unit, inv_std = norm_forward(
        layer_input[at].astype(jnp.float32) + (total + out_bias[...]), gain[...], offset[...]
    )
    low_value = normed.astype(jnp.bfloat16)
    unit_out[at] = unit
    inv_out[at] = jnp.broadcast_to(inv_std, (inv_std.shape[0], 128))
    low_out[at] = low_value
    return low_value


def middle_two(c, at, total, side, outs):
    low_in, bias, gain, offset, upstream = side
    output, resid_out, small = outs
    result, unit, inv_std = norm_forward(
        low_in[at].astype(jnp.float32) + (total + bias[...]), gain[...], offset[...]
    )
    output[at] = result.astype(jnp.bfloat16)
    grad_top = upstream[at].astype(jnp.float32)
    resid = norm_backward(grad_top, unit, inv_std, gain[...])
    resid_out[at] = resid
    branch = resid.astype(jnp.bfloat16)
    add_small(small, c, (grad_top * unit, grad_top, branch.astype(jnp.float32)))
    return branch


def middle_three(c, at, total, side, outs):
    resid_two, unit_one, inv_one, gain = side
    resid_out, small = outs
    grad_normed = total + resid_two[at]
    unit = unit_one[at]
    resid = norm_backward(grad_normed, unit, inv_one[at, 0:1], gain[...])
    resid_out[at] = resid
    branch = resid.astype(jnp.bfloat16)
    add_small(small, c, (grad_normed * unit, grad_normed, branch.astype(jnp.float32)))
    return branch


def place():
    p = lax.axis_index("dp")
    return p, lax.div(p, 2), lax.rem(p, 2), lax.axis_index("tensor")


def send_to(src, dst, send, recv, **peer):
    return pltpu.make_async_remote_copy(
        src_ref=src, dst_ref=dst, send_sem=send, recv_sem=recv, device_id=peer, device_id_type=MESH
    )


def greet_dp(barrier, groups, q, core):
    def signal(peer):
        pl.semaphore_signal(barrier, inc=1, device_id={"dp": peer}, device_id_type=MESH)

    signal(2 * q + 1 - core)

    def one(j, carry):
        signal(2 * lax.rem(q + j, groups) + core)
        return carry

    lax.fori_loop(1, groups, one, 0)


def opening_kernel(n, groups, x, first, second, x_full, first_full, second_full, *sems):
    p, q, core, z = place()
    send, recv, straight, pair, passed, from_peer, from_pair = sems
    weights = ((first, first_full), (second, second_full))
    barrier = pltpu.get_barrier_semaphore()
    greet_dp(barrier, groups, q, core)
    for there, other in ((z > 0, z - 1), (z < n - 1, z + 1)):

        @pl.when(there)
        def _():
            pl.semaphore_signal(barrier, inc=1, device_id={"tensor": other}, device_id_type=MESH)

    inner = (z > 0) & (z < n - 1)

    @pl.when(inner)
    def _():
        pl.semaphore_wait(barrier, groups + 2)

    @pl.when(jnp.logical_not(inner))
    def _():
        pl.semaphore_wait(barrier, groups + 1)

    def to_peer(w, j):
        shard, full = weights[w]
        peer = 2 * lax.rem(q + j, groups) + core
        return send_to(shard, full.at[p], straight.at[w, j], from_peer.at[w, q], dp=peer)

    def came(w, other):
        shard, full = weights[w]
        return send_to(
            shard, full.at[2 * other + core], straight.at[w, 0], from_peer.at[w, other], dp=2 * q + 1 - core
        )

    def to_pair(w, other):
        full = weights[w][1]
        block = full.at[2 * other + core]
        return send_to(block, block, passed.at[w, other], from_pair.at[w, other], dp=2 * q + 1 - core)

    def own_to_pair(w):
        shard, full = weights[w]
        return send_to(shard, full.at[p], pair.at[w], from_pair.at[w, q], dp=2 * q + 1 - core)

    def pair_came(w, other):
        shard, full = weights[w]
        return send_to(
            shard, full.at[2 * other + 1 - core], pair.at[w], from_pair.at[w, other], dp=2 * q + 1 - core
        )

    gather = LineGather(z, n, x_full, send, recv)
    x_full[z] = x[...]
    for c in range(row_chunks):
        gather.start(c)
    for w in range(2):

        def push(j, carry):
            to_peer(w, j).start()
            return carry

        lax.fori_loop(1, groups, push, 0)
        own_to_pair(w).start()
    for w in range(2):
        shard, full = weights[w]
        full[p] = shard[...]
    for c in range(row_chunks):
        gather.forward(c)
    for w in range(2):

        def forward(j, carry):
            other = lax.rem(q + groups - j, groups)
            came(w, other).wait_recv()
            to_pair(w, other).start()
            return carry

        lax.fori_loop(1, groups, forward, 0)
    for w in range(2):

        def collect(other, carry):
            pair_came(w, other).wait_recv()
            return carry

        lax.fori_loop(0, groups, collect, 0)

        def drain(j, carry):
            to_peer(w, j).wait_send()
            to_pair(w, lax.rem(q + groups - j, groups)).wait_send()
            return carry

        lax.fori_loop(1, groups, drain, 0)
        own_to_pair(w).wait_send()
    gather.drain()


def opening(n, devices, x, first, second):
    groups = devices // 2
    dma = pltpu.SemaphoreType.DMA
    low = jnp.bfloat16
    return pl.pallas_call(
        functools.partial(opening_kernel, n, groups),
        out_shape=[
            jax.ShapeDtypeStruct((n,) + x.shape, low),
            jax.ShapeDtypeStruct((devices,) + first.shape, low),
            jax.ShapeDtypeStruct((devices,) + second.shape, low),
        ],
        in_specs=[in_vmem] * 3,
        out_specs=[in_vmem] * 3,
        scratch_shapes=[
            dma((2, n, row_chunks)),
            dma((n, row_chunks)),
            dma((2, groups)),
            dma((2,)),
            dma((2, groups)),
            dma((2, groups)),
            dma((2, groups)),
        ],
        compiler_params=pltpu.CompilerParams(
            collective_id=4, has_side_effects=True, vmem_limit_bytes=32 * 1024 * 1024
        ),
        cost_estimate=pl.CostEstimate(flops=60000000, bytes_accessed=40000000, transcendentals=0),
        name="opening",
    )(x, first, second)


def closing_kernel(n, groups, part, resid, grads, small, grad_input, total, small_all, *scratch):
    stage, from_left, from_right, acc, pair_buf, mine, peer_buf, small_pair, small_sum = scratch[:9]
    (
        sum_send, sum_recv, pair_send, pair_recv, peer_send, peer_recv,
        small_pair_send, small_pair_recv, small_send, small_recv, end_send, end_recv,
    ) = scratch[9:]
    p, q, core, z = place()
    barrier = pltpu.get_barrier_semaphore()
    greet_dp(barrier, groups, q, core)
    for k in range(1, n):
        pl.semaphore_signal(
            barrier, inc=1, device_id={"tensor": lax.rem(z + k, n)}, device_id_type=MESH
        )
    pl.semaphore_wait(barrier, groups + n - 1)
    sibling = 2 * q + 1 - core

    def to_pair(other):
        return send_to(
            grads.at[2 * other + 1 - core], pair_buf.at[other], pair_send.at[other], pair_recv.at[other], dp=sibling
        )

    def to_peer(other):
        return send_to(
            mine.at[other], peer_buf.at[q], peer_send.at[other], peer_recv.at[q], dp=2 * other + core
        )

    def from_peer(other):
        return send_to(
            mine.at[other], peer_buf.at[other], peer_send.at[other], peer_recv.at[other], dp=2 * other + core
        )

    def small_to_peer(other):
        return send_to(
            small_sum.at[q], small_sum.at[q], small_send.at[other], small_recv.at[q], dp=2 * other + core
        )

    def small_from_peer(other):
        return send_to(
            small_sum.at[other], small_sum.at[other], small_send.at[other], small_recv.at[other], dp=2 * other + core
        )

    def small_on(k):
        there = lax.rem(z + k, n)
        return send_to(small_all.at[z], small_all.at[z], end_send.at[k], end_recv.at[z], tensor=there)

    def small_came(k):
        there = lax.rem(z + k, n)
        return send_to(small_all.at[there], small_all.at[there], end_send.at[k], end_recv.at[there], tensor=there)

    def others(body):
        def one(j, carry):
            body(lax.rem(q + j, groups))
            return carry

        lax.fori_loop(1, groups, one, 0)

    small_pair_copy = send_to(small, small_pair, small_pair_send, small_pair_recv, dp=sibling)
    small_pair_copy.start()
    others(lambda other: to_pair(other).start())
    to_pair(q).start()
    line = LineSum(z, n, part, stage, from_left, from_right, acc, sum_send, sum_recv)
    line.start_ends()
    small_pair_copy.wait_recv()
    small_sum[q] = small[...] + small_pair[...]
    others(lambda other: small_to_peer(other).start())

    def pass_on(other):
        to_pair(other).wait_recv()
        pair_total = grads[2 * other + core].astype(jnp.float32) + pair_buf[other].astype(jnp.float32)
        mine[other] = pair_total.astype(jnp.bfloat16)
        to_peer(other).start()

    others(pass_on)
    line.forward(0)
    line.forward(1)
    others(lambda other: small_from_peer(other).wait_recv())
    plane = small_sum[0]
    for other in range(1, groups):
        plane = plane + small_sum[other]
    small_all[z] = plane
    for k in range(1, n):
        small_on(k).start()
    for c in range(row_chunks):
        if c + 2 < row_chunks:
            line.forward(c + 2)
        at = line.at(c)
        grad_input[at] = (line.finish(c) + resid[at]).astype(jnp.bfloat16)
    to_pair(q).wait_recv()
    total[...] = grads[p].astype(jnp.float32) + pair_buf[q].astype(jnp.float32)

    def add_peer(other):
        from_peer(other).wait_recv()
        total[...] += peer_buf[other].astype(jnp.float32)

    others(add_peer)
    for k in range(1, n):
        small_came(k).wait_recv()
    line.drain()
    small_pair_copy.wait_send()
    to_pair(q).wait_send()

    def drain(other):
        to_pair(other).wait_send()
        to_peer(other).wait_send()
        small_to_peer(other).wait_send()

    others(drain)
    for k in range(1, n):
        small_on(k).wait_send()


def closing(n, devices, part, resid, grads, small):
    groups = devices // 2
    dma = pltpu.SemaphoreType.DMA
    low, wide = jnp.bfloat16, jnp.float32
    slab = grads.shape[1:]
    return pl.pallas_call(
        functools.partial(closing_kernel, n, groups),
        out_shape=[
            jax.ShapeDtypeStruct(resid.shape, low),
            jax.ShapeDtypeStruct(slab, wide),
            jax.ShapeDtypeStruct((n,) + small.shape, wide),
        ],
        in_specs=[in_vmem] * 4,
        out_specs=[in_vmem] * 3,
        scratch_shapes=[pltpu.VMEM(part.shape, low)] * 3
        + [
            pltpu.VMEM(part.shape[1:], wide),
            pltpu.VMEM((groups,) + slab, low),
            pltpu.VMEM((groups,) + slab, low),
            pltpu.VMEM((groups,) + slab, low),
            pltpu.VMEM(small.shape, wide),
            pltpu.VMEM((groups,) + small.shape, wide),
            dma((2, n, row_chunks)),
            dma((2, n, row_chunks)),
            dma((groups,)),
            dma((groups,)),
            dma((groups,)),
            dma((groups,)),
            dma(()),
            dma(()),
            dma((groups,)),
            dma((groups,)),
            dma((n,)),
            dma((n,)),
        ],
        compiler_params=pltpu.CompilerParams(
            collective_id=5, has_side_effects=True, vmem_limit_bytes=32 * 1024 * 1024
        ),
        cost_estimate=pl.CostEstimate(flops=60000000, bytes_accessed=40000000, transcendentals=0),
        name="closing",
    )(part, resid, grads, small)


def attend(operands):
    queries, key_rows, values = operands
    scores = jnp.einsum(
        "qhe,khe->hqk", queries, key_rows, preferred_element_type=jnp.float32
    ) * HD ** (-0.5)
    row_max = jnp.max(scores, axis=-1, keepdims=True)
    shifted = jnp.exp(scores - row_max)
    row_total = jnp.sum(shifted, axis=-1, keepdims=True)
    probs = (shifted / row_total).astype(jnp.bfloat16)
    attended = jnp.einsum("hqk,khe->qhe", probs, values, preferred_element_type=jnp.float32).astype(
        jnp.bfloat16
    )
    return (attended, row_max + jnp.log(row_total))


def attend_back(operands):
    queries, key_rows, values, log_total, grad_attended = operands
    scores = jnp.einsum(
        "qhe,khe->hqk", queries, key_rows, preferred_element_type=jnp.float32
    ) * HD ** (-0.5)
    probs = jnp.exp(scores - log_total)
    grad_probs = jnp.einsum(
        "qhe,khe->hqk", grad_attended, values, preferred_element_type=jnp.float32
    )
    grad_values = jnp.einsum(
        "hqk,qhe->khe",
        probs.astype(jnp.bfloat16),
        grad_attended,
        preferred_element_type=jnp.float32,
    ).astype(jnp.bfloat16)
    row_dot = jnp.sum(probs * grad_probs, axis=-1, keepdims=True)
    grad_scores = (probs * (grad_probs - row_dot)).astype(jnp.bfloat16)
    grad_queries = (
        jnp.einsum("hqk,khe->qhe", grad_scores, key_rows, preferred_element_type=jnp.float32)
        * HD ** (-0.5)
    ).astype(jnp.bfloat16)
    grad_keys = (
        jnp.einsum("hqk,qhe->khe", grad_scores, queries, preferred_element_type=jnp.float32)
        * HD ** (-0.5)
    ).astype(jnp.bfloat16)
    return (grad_queries, grad_keys, grad_values)


def body(
    layer_input,
    qkv_weight,
    query_bias,
    value_bias,
    out_weight,
    out_bias,
    attn_norm_gain,
    attn_norm_bias,
    ffn_in_weight,
    ffn_in_bias,
    ffn_out_weight,
    ffn_out_bias,
    ffn_norm_gain,
    ffn_norm_bias,
    grad_output,
):
    tensor_parts = lax.axis_size("tensor")
    tensor_rank = lax.axis_index("tensor")
    heads_here = HEADS // tensor_parts
    width_here = heads_here * HD
    hidden_here = FF // tensor_parts
    dp_parts = lax.axis_size("dp")
    ffn_in_full, ffn_out_full = (
        lax.all_gather(ffn_in_weight, "dp", axis=0, tiled=True),
        lax.all_gather(ffn_out_weight, "dp", axis=1, tiled=True),
    )
    seq_count, piece_len, feature_count = layer_input.shape
    length = piece_len * tensor_parts
    row_count = seq_count * length
    local_rows = seq_count * piece_len

    def by_piece(rows):
        rows = rows.astype(jnp.bfloat16).reshape(seq_count, tensor_parts, piece_len, feature_count)
        return rows.swapaxes(0, 1).reshape(tensor_parts, local_rows, feature_count)

    def by_row(pieces):
        pieces = pieces.reshape(tensor_parts, seq_count, piece_len, feature_count)
        return pieces.swapaxes(0, 1).reshape(row_count, feature_count)

    local_input = layer_input.reshape(local_rows, feature_count)
    input_pieces, qkv_slots, out_slots = opening(
        tensor_parts, dp_parts, local_input, qkv_weight, out_weight
    )
    input_rows = by_row(input_pieces)
    qkv_full = qkv_slots.reshape(feature_count, 3 * width_here)
    out_full = out_slots.swapaxes(0, 1).reshape(width_here, feature_count)
    packed = matmul(input_rows, qkv_full).reshape(seq_count, length, heads_here, 3, HD)
    query_slice = lax.dynamic_slice_in_dim(
        query_bias.reshape(HEADS, HD), tensor_rank * heads_here, heads_here, 0
    )
    value_slice = lax.dynamic_slice_in_dim(
        value_bias.reshape(HEADS, HD), tensor_rank * heads_here, heads_here, 0
    )
    queries = (packed[:, :, :, 0] + query_slice).astype(jnp.bfloat16)
    key_rows = packed[:, :, :, 1].astype(jnp.bfloat16)
    values = (packed[:, :, :, 2] + value_slice).astype(jnp.bfloat16)
    attended, log_total = lax.map(attend, (queries, key_rows, values))
    attended_rows = attended.reshape(row_count, width_here)
    wide = jax.ShapeDtypeStruct((local_rows, feature_count), jnp.float32)
    low = jax.ShapeDtypeStruct((local_rows, feature_count), jnp.bfloat16)
    sums = jax.ShapeDtypeStruct((3, feature_count), jnp.float32)
    normed_pieces, unit_one, inv_std_one, normed_low = turn(
        tensor_parts,
        1,
        "turn_one",
        middle_one,
        by_piece(matmul(attended_rows, out_full)),
        (local_input, out_bias[None], attn_norm_gain[None], attn_norm_bias[None]),
        [wide, jax.ShapeDtypeStruct((local_rows, 128), jnp.float32), low],
    )
    normed_rows = by_row(normed_pieces)
    inner_bias = lax.dynamic_slice_in_dim(ffn_in_bias, tensor_rank * hidden_here, hidden_here, 0)
    inner_pre = matmul(normed_rows, ffn_in_full) + inner_bias
    activated = gelu_exact(inner_pre).astype(jnp.bfloat16)
    branch_two_pieces, layer_output, grad_resid_two, small_two = turn(
        tensor_parts,
        2,
        "turn_two",
        middle_two,
        by_piece(matmul(activated, ffn_out_full)),
        (
            normed_low,
            ffn_out_bias[None],
            ffn_norm_gain[None],
            ffn_norm_bias[None],
            grad_output.reshape(local_rows, feature_count),
        ),
        [low, wide, sums],
    )
    layer_output = layer_output.reshape(layer_input.shape)
    grad_ffn_norm_gain, grad_ffn_norm_bias, grad_ffn_out_bias = small_two
    branch_two_rows = by_row(branch_two_pieces)
    grad_activated = matmul_by_transpose(branch_two_rows, ffn_out_full).astype(jnp.bfloat16)
    grad_ffn_out_local = transpose_matmul(branch_two_rows, activated)
    grad_inner = (grad_activated.astype(jnp.float32) * gelu_slope(inner_pre)).astype(jnp.bfloat16)
    inner_bias_grad = jnp.sum(grad_inner.astype(jnp.float32), axis=0)
    grad_ffn_in_local = transpose_matmul(normed_rows, grad_inner)
    shard_rows = feature_count // dp_parts
    ffn_local = jnp.concatenate(
        (
            grad_ffn_in_local.astype(jnp.bfloat16).reshape(dp_parts, shard_rows, hidden_here),
            grad_ffn_out_local.astype(jnp.bfloat16).reshape(dp_parts, shard_rows, hidden_here),
        ),
        axis=1,
    ).reshape(2 * feature_count, hidden_here)
    normed_part = by_piece(matmul_by_transpose(grad_inner, ffn_in_full))
    ffn_local, normed_part = lax.optimization_barrier((ffn_local, normed_part))
    ffn_grads = lax.psum_scatter(ffn_local, "dp", scatter_dimension=0, tiled=True).astype(jnp.float32)
    branch_one_pieces, grad_resid_one, small_one = turn(
        tensor_parts,
        3,
        "turn_three",
        middle_three,
        normed_part,
        (grad_resid_two, unit_one, inv_std_one, attn_norm_gain[None]),
        [wide, sums],
    )
    grad_attn_norm_gain, grad_attn_norm_bias, grad_out_bias = small_one
    branch_one_rows = by_row(branch_one_pieces)
    grad_attended = (
        matmul_by_transpose(branch_one_rows, out_full)
        .astype(jnp.bfloat16)
        .reshape(seq_count, length, heads_here, HD)
    )
    grad_out_local = transpose_matmul(branch_one_rows, attended_rows)
    grad_queries, grad_keys, grad_values = lax.map(
        attend_back, (queries, key_rows, values, log_total, grad_attended)
    )
    grad_packed = jnp.stack((grad_queries, grad_keys, grad_values), axis=3).reshape(
        row_count, 3 * width_here
    )
    grad_qkv_local = transpose_matmul(input_rows, grad_packed)
    query_grad_here = jnp.sum(grad_queries.astype(jnp.float32), axis=(0, 1)).reshape(width_here)
    value_grad_here = jnp.sum(grad_values.astype(jnp.float32), axis=(0, 1)).reshape(width_here)
    pieces = (
        query_grad_here,
        value_grad_here,
        inner_bias_grad,
        grad_out_bias,
        grad_attn_norm_gain,
        grad_attn_norm_bias,
        grad_ffn_out_bias,
        grad_ffn_norm_gain,
        grad_ffn_norm_bias,
    )
    small_size = sum(piece.shape[0] for piece in pieces)
    small = jnp.pad(jnp.concatenate(pieces), (0, -small_size % 1024)).reshape(-1, 128)
    attn_local = jnp.concatenate(
        (grad_qkv_local.astype(jnp.bfloat16), grad_out_local.astype(jnp.bfloat16)), axis=1
    ).reshape(dp_parts, shard_rows, 4 * width_here)
    grad_input, attn_grads, small_all = closing(
        tensor_parts,
        dp_parts,
        by_piece(matmul_by_transpose(grad_packed, qkv_full)),
        grad_resid_one,
        attn_local,
        small,
    )
    grad_input = grad_input.reshape(layer_input.shape)
    grad_ffn_in_weight = ffn_grads[:shard_rows]
    grad_ffn_out_weight = ffn_grads[shard_rows:].T
    grad_qkv_weight = attn_grads[:, : 3 * width_here]
    grad_out_weight = attn_grads[:, 3 * width_here :].T
    flat = small_all.reshape(tensor_parts, -1)
    split = 2 * width_here + hidden_here
    common = jnp.sum(flat[:, split:small_size], axis=0).reshape(6, feature_count)
    summed = (
        flat[:, :width_here].reshape(-1),
        flat[:, width_here : 2 * width_here].reshape(-1),
        common[0],
        common[1],
        common[2],
        flat[:, 2 * width_here : split].reshape(-1),
        common[3],
        common[4],
        common[5],
    )
    return (
        layer_output,
        grad_input,
        grad_qkv_weight,
        summed[0],
        summed[1],
        grad_out_weight,
        summed[2],
        summed[3],
        summed[4],
        grad_ffn_in_weight,
        summed[5],
        grad_ffn_out_weight,
        summed[6],
        summed[7],
        summed[8],
    )


def solution(mesh):
    placed = (
        P("dp", "tensor", None),
        P("dp", "tensor"),
        P(),
        P(),
        P("tensor", "dp"),
        P(),
        P(),
        P(),
        P("dp", "tensor"),
        P(),
        P("tensor", "dp"),
        P(),
        P(),
        P(),
        P("dp", "tensor", None),
    )
    return jax.shard_map(
        body,
        mesh=mesh,
        in_specs=placed,
        out_specs=(
            P("dp", "tensor", None),
            P("dp", "tensor", None),
            P("dp", "tensor"),
            P(),
            P(),
            P("tensor", "dp"),
            P(),
            P(),
            P(),
            P("dp", "tensor"),
            P(),
            P("tensor", "dp"),
            P(),
            P(),
            P(),
        ),
        check_vma=False,
    )
```

```python
import functools

import jax
import jax.numpy as jnp
from jax import lax
from jax.experimental import pallas as pl
from jax.experimental.pallas import tpu as pltpu
from jax.sharding import PartitionSpec as P

HEADS = 16
HD = 64
FF = 4096


norm_eps = 1e-05
root_half = 0.7071067811865476
inv_root_tau = 0.3989422804014327


def matmul(first_op, second_op):
    return jnp.dot(first_op, second_op, preferred_element_type=jnp.float32)


def matmul_by_transpose(first_op, second_op):
    return lax.dot_general(
        first_op, second_op, (((1,), (1,)), ((), ())), preferred_element_type=jnp.float32
    )


def transpose_matmul(first_op, second_op):
    return lax.dot_general(
        first_op, second_op, (((0,), (0,)), ((), ())), preferred_element_type=jnp.float32
    )


def norm_forward(residual, norm_gain, offset):
    center = residual - jnp.mean(residual, axis=-1, keepdims=True)
    variance = jnp.mean(center * center, axis=-1, keepdims=True)
    inv_std = lax.rsqrt(variance + norm_eps)
    normed = center * inv_std
    return (normed * norm_gain + offset, normed, inv_std)


def norm_backward(upstream, normed, inv_std, norm_gain):
    scaled = upstream * norm_gain
    centered = scaled - jnp.mean(scaled, axis=-1, keepdims=True)
    return inv_std * (centered - normed * jnp.mean(scaled * normed, axis=-1, keepdims=True))


def gelu_exact(preact):
    return 0.5 * preact * (1.0 + lax.erf(preact * root_half))


def gelu_slope(preact):
    return (
        0.5 * (1.0 + lax.erf(preact * root_half))
        + preact * jnp.exp(-0.5 * preact * preact) * inv_root_tau
    )


MESH = pl.DeviceIdType.MESH
in_vmem = pl.BlockSpec(memory_space=pltpu.VMEM)
row_chunks = 2


def line_barrier(z, n):
    barrier = pltpu.get_barrier_semaphore()
    for there, other in ((z > 0, z - 1), (z < n - 1, z + 1)):

        @pl.when(there)
        def _():
            pl.semaphore_signal(barrier, inc=1, device_id={"tensor": other}, device_id_type=MESH)

    inner = (z > 0) & (z < n - 1)

    @pl.when(inner)
    def _():
        pl.semaphore_wait(barrier, 2)

    @pl.when(jnp.logical_not(inner))
    def _():
        pl.semaphore_wait(barrier, 1)


class LineSum:
    def __init__(self, z, n, part, stage, from_left, from_right, acc, send, recv):
        self.z, self.n = z, n
        self.part, self.stage, self.acc = part, stage, acc
        self.bufs, self.send, self.recv = (from_left, from_right), send, recv
        self.rows = part.shape[1] // row_chunks

    def at(self, c):
        return pl.ds(c * self.rows, self.rows)

    def copy(self, way, d, c, src):
        z, n = self.z, self.n
        other = lax.rem(z + 1, n) if way == 0 else lax.rem(z + n - 1, n)
        return pltpu.make_async_remote_copy(
            src_ref=src.at[d, self.at(c)],
            dst_ref=self.bufs[way].at[d, self.at(c)],
            send_sem=self.send.at[way, d, c],
            recv_sem=self.recv.at[way, d, c],
            device_id={"tensor": other},
            device_id_type=MESH,
        )

    def pairs(self):
        for k in range(self.n - 1):
            yield 0, self.n - 1 - k, self.z < self.n - 1 - k
            yield 1, k, self.z > k

    def start_ends(self):
        for c in range(row_chunks):
            for way, d, active in self.pairs():

                @pl.when(self.z == (0 if way == 0 else self.n - 1))
                def _():
                    self.copy(way, d, c, self.part).start()

    def forward(self, c):
        near_left = self.z < self.n // 2
        self.forward_way(0, c, near_left)
        self.forward_way(1, c, self.z >= 0)
        self.forward_way(0, c, jnp.logical_not(near_left))

    def forward_way(self, wanted, c, now):
        for way, d, active in self.pairs():
            if way != wanted:
                continue
            inner = self.z > 0 if way == 0 else self.z < self.n - 1

            @pl.when(active & inner & now)
            def _():
                self.copy(way, d, c, self.part).wait_recv()
                at = self.at(c)
                total = self.part[d, at].astype(jnp.float32) + self.bufs[way][d, at].astype(jnp.float32)
                self.stage[d, at] = total.astype(jnp.bfloat16)
                self.copy(way, d, c, self.stage).start()

    def finish(self, c):
        z, at = self.z, self.at(c)
        self.acc[at] = self.part[z, at].astype(jnp.float32)
        for way, there in ((0, z > 0), (1, z < self.n - 1)):

            @pl.when(there)
            def _():
                self.copy(way, z, c, self.part).wait_recv()
                self.acc[at] += self.bufs[way][z, at].astype(jnp.float32)

        return self.acc[at]

    def drain(self):
        for c in range(row_chunks):
            for way, d, active in self.pairs():

                @pl.when(active)
                def _():
                    self.copy(way, d, c, self.part).wait_send()


class LineGather:
    def __init__(self, z, n, full, send, recv):
        self.z, self.n, self.full, self.send, self.recv = z, n, full, send, recv
        self.rows = full.shape[1] // row_chunks

    def copy(self, way, s, c):
        z, n = self.z, self.n
        other = lax.rem(z + 1, n) if way == 0 else lax.rem(z + n - 1, n)
        block = self.full.at[s, pl.ds(c * self.rows, self.rows)]
        return pltpu.make_async_remote_copy(
            src_ref=block,
            dst_ref=block,
            send_sem=self.send.at[way, s, c],
            recv_sem=self.recv.at[s, c],
            device_id={"tensor": other},
            device_id_type=MESH,
        )

    def start(self, c):
        for way, there in ((0, self.z < self.n - 1), (1, self.z > 0)):

            @pl.when(there)
            def _():
                self.copy(way, self.z, c).start()

    def forward(self, c):
        for k in range(1, self.n):
            for way, s, there, onward in (
                (0, self.z - k, self.z >= k, self.z < self.n - 1),
                (1, self.z + k, self.z < self.n - k, self.z > 0),
            ):

                @pl.when(there)
                def _():
                    self.copy(way, s, c).wait_recv()

                    @pl.when(onward)
                    def _():
                        self.copy(way, s, c).start()

    def drain(self):
        for c in range(row_chunks):
            for s in range(self.n):
                for way, sent in (
                    (0, (self.z >= s) & (self.z < self.n - 1)),
                    (1, (self.z <= s) & (self.z > 0)),
                ):

                    @pl.when(sent)
                    def _():
                        self.copy(way, s, c).wait_send()


def turn_kernel(n, middle, side_count, out_count, *refs):
    part, side = refs[0], refs[1 : 1 + side_count]
    full, outs = refs[1 + side_count], refs[2 + side_count : 2 + side_count + out_count]
    stage, from_left, from_right, acc, sum_send, sum_recv, send, recv = refs[2 + side_count + out_count :]
    z = lax.axis_index("tensor")
    line_barrier(z, n)
    summing = LineSum(z, n, part, stage, from_left, from_right, acc, sum_send, sum_recv)
    gather = LineGather(z, n, full, send, recv)
    summing.start_ends()
    summing.forward(0)
    for c in range(row_chunks):
        if c + 1 < row_chunks:
            summing.forward(c + 1)
        total = summing.finish(c)
        full[z, summing.at(c)] = middle(c, summing.at(c), total, side, outs)
        gather.start(c)
        if c > 0:
            gather.forward(c - 1)
    gather.forward(row_chunks - 1)
    summing.drain()
    gather.drain()


def turn(n, number, name, middle, part, side, out_shapes):
    shape = part.shape
    return pl.pallas_call(
        functools.partial(turn_kernel, n, middle, len(side), len(out_shapes)),
        out_shape=[jax.ShapeDtypeStruct(shape, jnp.bfloat16)] + out_shapes,
        in_specs=[in_vmem] * (1 + len(side)),
        out_specs=[in_vmem] * (1 + len(out_shapes)),
        scratch_shapes=[pltpu.VMEM(shape, jnp.bfloat16)] * 3
        + [
            pltpu.VMEM(shape[1:], jnp.float32),
            pltpu.SemaphoreType.DMA((2, n, row_chunks)),
            pltpu.SemaphoreType.DMA((2, n, row_chunks)),
            pltpu.SemaphoreType.DMA((2, n, row_chunks)),
            pltpu.SemaphoreType.DMA((n, row_chunks)),
        ],
        compiler_params=pltpu.CompilerParams(
            collective_id=number, has_side_effects=True, vmem_limit_bytes=32 * 1024 * 1024
        ),
        cost_estimate=pl.CostEstimate(flops=60000000, bytes_accessed=40000000, transcendentals=0),
        name=name,
    )(part, *side)


def add_small(ref, c, values):
    for i, value in enumerate(values):
        row = jnp.sum(value, axis=0, keepdims=True)
        ref[i : i + 1] = row if c == 0 else ref[i : i + 1] + row


def middle_one(c, at, total, side, outs):
    layer_input, out_bias, gain, offset = side
    unit_out, inv_out, low_out = outs
    normed, unit, inv_std = norm_forward(
        layer_input[at].astype(jnp.float32) + (total + out_bias[...]), gain[...], offset[...]
    )
    low_value = normed.astype(jnp.bfloat16)
    unit_out[at] = unit
    inv_out[at] = jnp.broadcast_to(inv_std, (inv_std.shape[0], 128))
    low_out[at] = low_value
    return low_value


def middle_two(c, at, total, side, outs):
    low_in, bias, gain, offset, upstream = side
    output, resid_out, small = outs
    result, unit, inv_std = norm_forward(
        low_in[at].astype(jnp.float32) + (total + bias[...]), gain[...], offset[...]
    )
    output[at] = result.astype(jnp.bfloat16)
    grad_top = upstream[at].astype(jnp.float32)
    resid = norm_backward(grad_top, unit, inv_std, gain[...])
    resid_out[at] = resid
    branch = resid.astype(jnp.bfloat16)
    add_small(small, c, (grad_top * unit, grad_top, branch.astype(jnp.float32)))
    return branch


def middle_three(c, at, total, side, outs):
    resid_two, unit_one, inv_one, gain = side
    resid_out, small = outs
    grad_normed = total + resid_two[at]
    unit = unit_one[at]
    resid = norm_backward(grad_normed, unit, inv_one[at, 0:1], gain[...])
    resid_out[at] = resid
    branch = resid.astype(jnp.bfloat16)
    add_small(small, c, (grad_normed * unit, grad_normed, branch.astype(jnp.float32)))
    return branch


def place():
    p = lax.axis_index("dp")
    return p, lax.div(p, 2), lax.rem(p, 2), lax.axis_index("tensor")


def send_to(src, dst, send, recv, **peer):
    return pltpu.make_async_remote_copy(
        src_ref=src, dst_ref=dst, send_sem=send, recv_sem=recv, device_id=peer, device_id_type=MESH
    )


def greet_dp(barrier, groups, q, core):
    def signal(peer):
        pl.semaphore_signal(barrier, inc=1, device_id={"dp": peer}, device_id_type=MESH)

    signal(2 * q + 1 - core)

    def one(j, carry):
        signal(2 * lax.rem(q + j, groups) + core)
        return carry

    lax.fori_loop(1, groups, one, 0)


def opening_kernel(n, groups, x, first, second, x_full, first_full, second_full, *sems):
    p, q, core, z = place()
    send, recv, straight, pair, passed, from_peer, from_pair = sems
    weights = ((first, first_full), (second, second_full))
    barrier = pltpu.get_barrier_semaphore()
    greet_dp(barrier, groups, q, core)
    for there, other in ((z > 0, z - 1), (z < n - 1, z + 1)):

        @pl.when(there)
        def _():
            pl.semaphore_signal(barrier, inc=1, device_id={"tensor": other}, device_id_type=MESH)

    inner = (z > 0) & (z < n - 1)

    @pl.when(inner)
    def _():
        pl.semaphore_wait(barrier, groups + 2)

    @pl.when(jnp.logical_not(inner))
    def _():
        pl.semaphore_wait(barrier, groups + 1)

    def to_peer(w, j):
        shard, full = weights[w]
        peer = 2 * lax.rem(q + j, groups) + core
        return send_to(shard, full.at[p], straight.at[w, j], from_peer.at[w, q], dp=peer)

    def came(w, other):
        shard, full = weights[w]
        return send_to(
            shard, full.at[2 * other + core], straight.at[w, 0], from_peer.at[w, other], dp=2 * q + 1 - core
        )

    def to_pair(w, other):
        full = weights[w][1]
        block = full.at[2 * other + core]
        return send_to(block, block, passed.at[w, other], from_pair.at[w, other], dp=2 * q + 1 - core)

    def own_to_pair(w):
        shard, full = weights[w]
        return send_to(shard, full.at[p], pair.at[w], from_pair.at[w, q], dp=2 * q + 1 - core)

    def pair_came(w, other):
        shard, full = weights[w]
        return send_to(
            shard, full.at[2 * other + 1 - core], pair.at[w], from_pair.at[w, other], dp=2 * q + 1 - core
        )

    gather = LineGather(z, n, x_full, send, recv)
    x_full[z] = x[...]
    for c in range(row_chunks):
        gather.start(c)
    for w in range(2):

        def push(j, carry):
            to_peer(w, j).start()
            return carry

        lax.fori_loop(1, groups, push, 0)
        own_to_pair(w).start()
    for w in range(2):
        shard, full = weights[w]
        full[p] = shard[...]
    for c in range(row_chunks):
        gather.forward(c)
    for w in range(2):

        def forward(j, carry):
            other = lax.rem(q + groups - j, groups)
            came(w, other).wait_recv()
            to_pair(w, other).start()
            return carry

        lax.fori_loop(1, groups, forward, 0)
    for w in range(2):

        def collect(other, carry):
            pair_came(w, other).wait_recv()
            return carry

        lax.fori_loop(0, groups, collect, 0)

        def drain(j, carry):
            to_peer(w, j).wait_send()
            to_pair(w, lax.rem(q + groups - j, groups)).wait_send()
            return carry

        lax.fori_loop(1, groups, drain, 0)
        own_to_pair(w).wait_send()
    gather.drain()


def opening(n, devices, x, first, second):
    groups = devices // 2
    dma = pltpu.SemaphoreType.DMA
    low = jnp.bfloat16
    return pl.pallas_call(
        functools.partial(opening_kernel, n, groups),
        out_shape=[
            jax.ShapeDtypeStruct((n,) + x.shape, low),
            jax.ShapeDtypeStruct((devices,) + first.shape, low),
            jax.ShapeDtypeStruct((devices,) + second.shape, low),
        ],
        in_specs=[in_vmem] * 3,
        out_specs=[in_vmem] * 3,
        scratch_shapes=[
            dma((2, n, row_chunks)),
            dma((n, row_chunks)),
            dma((2, groups)),
            dma((2,)),
            dma((2, groups)),
            dma((2, groups)),
            dma((2, groups)),
        ],
        compiler_params=pltpu.CompilerParams(
            collective_id=4, has_side_effects=True, vmem_limit_bytes=32 * 1024 * 1024
        ),
        cost_estimate=pl.CostEstimate(flops=60000000, bytes_accessed=40000000, transcendentals=0),
        name="opening",
    )(x, first, second)


def closing_kernel(n, groups, part, resid, grads, small, grad_input, total, small_all, *scratch):
    stage, from_left, from_right, acc, pair_buf, mine, peer_buf, small_pair, small_sum = scratch[:9]
    (
        sum_send, sum_recv, pair_send, pair_recv, peer_send, peer_recv,
        small_pair_send, small_pair_recv, small_send, small_recv, end_send, end_recv,
    ) = scratch[9:]
    p, q, core, z = place()
    barrier = pltpu.get_barrier_semaphore()
    greet_dp(barrier, groups, q, core)
    for k in range(1, n):
        pl.semaphore_signal(
            barrier, inc=1, device_id={"tensor": lax.rem(z + k, n)}, device_id_type=MESH
        )
    pl.semaphore_wait(barrier, groups + n - 1)
    sibling = 2 * q + 1 - core

    def to_pair(other):
        return send_to(
            grads.at[2 * other + 1 - core], pair_buf.at[other], pair_send.at[other], pair_recv.at[other], dp=sibling
        )

    def to_peer(other):
        return send_to(
            mine.at[other], peer_buf.at[q], peer_send.at[other], peer_recv.at[q], dp=2 * other + core
        )

    def from_peer(other):
        return send_to(
            mine.at[other], peer_buf.at[other], peer_send.at[other], peer_recv.at[other], dp=2 * other + core
        )

    def small_to_peer(other):
        return send_to(
            small_sum.at[q], small_sum.at[q], small_send.at[other], small_recv.at[q], dp=2 * other + core
        )

    def small_from_peer(other):
        return send_to(
            small_sum.at[other], small_sum.at[other], small_send.at[other], small_recv.at[other], dp=2 * other + core
        )

    def small_on(k):
        there = lax.rem(z + k, n)
        return send_to(small_all.at[z], small_all.at[z], end_send.at[k], end_recv.at[z], tensor=there)

    def small_came(k):
        there = lax.rem(z + k, n)
        return send_to(small_all.at[there], small_all.at[there], end_send.at[k], end_recv.at[there], tensor=there)

    def others(body):
        def one(j, carry):
            body(lax.rem(q + j, groups))
            return carry

        lax.fori_loop(1, groups, one, 0)

    small_pair_copy = send_to(small, small_pair, small_pair_send, small_pair_recv, dp=sibling)
    small_pair_copy.start()
    others(lambda other: to_pair(other).start())
    to_pair(q).start()
    line = LineSum(z, n, part, stage, from_left, from_right, acc, sum_send, sum_recv)
    line.start_ends()
    small_pair_copy.wait_recv()
    small_sum[q] = small[...] + small_pair[...]
    others(lambda other: small_to_peer(other).start())

    def pass_on(other):
        to_pair(other).wait_recv()
        pair_total = grads[2 * other + core].astype(jnp.float32) + pair_buf[other].astype(jnp.float32)
        mine[other] = pair_total.astype(jnp.bfloat16)
        to_peer(other).start()

    others(pass_on)
    line.forward(0)
    line.forward(1)
    others(lambda other: small_from_peer(other).wait_recv())
    plane = small_sum[0]
    for other in range(1, groups):
        plane = plane + small_sum[other]
    small_all[z] = plane
    for k in range(1, n):
        small_on(k).start()
    for c in range(row_chunks):
        if c + 2 < row_chunks:
            line.forward(c + 2)
        at = line.at(c)
        grad_input[at] = (line.finish(c) + resid[at]).astype(jnp.bfloat16)
    to_pair(q).wait_recv()
    total[...] = grads[p].astype(jnp.float32) + pair_buf[q].astype(jnp.float32)

    def add_peer(other):
        from_peer(other).wait_recv()
        total[...] += peer_buf[other].astype(jnp.float32)

    others(add_peer)
    for k in range(1, n):
        small_came(k).wait_recv()
    line.drain()
    small_pair_copy.wait_send()
    to_pair(q).wait_send()

    def drain(other):
        to_pair(other).wait_send()
        to_peer(other).wait_send()
        small_to_peer(other).wait_send()

    others(drain)
    for k in range(1, n):
        small_on(k).wait_send()


def closing(n, devices, part, resid, grads, small):
    groups = devices // 2
    dma = pltpu.SemaphoreType.DMA
    low, wide = jnp.bfloat16, jnp.float32
    slab = grads.shape[1:]
    return pl.pallas_call(
        functools.partial(closing_kernel, n, groups),
        out_shape=[
            jax.ShapeDtypeStruct(resid.shape, low),
            jax.ShapeDtypeStruct(slab, wide),
            jax.ShapeDtypeStruct((n,) + small.shape, wide),
        ],
        in_specs=[in_vmem] * 4,
        out_specs=[in_vmem] * 3,
        scratch_shapes=[pltpu.VMEM(part.shape, low)] * 3
        + [
            pltpu.VMEM(part.shape[1:], wide),
            pltpu.VMEM((groups,) + slab, low),
            pltpu.VMEM((groups,) + slab, low),
            pltpu.VMEM((groups,) + slab, low),
            pltpu.VMEM(small.shape, wide),
            pltpu.VMEM((groups,) + small.shape, wide),
            dma((2, n, row_chunks)),
            dma((2, n, row_chunks)),
            dma((groups,)),
            dma((groups,)),
            dma((groups,)),
            dma((groups,)),
            dma(()),
            dma(()),
            dma((groups,)),
            dma((groups,)),
            dma((n,)),
            dma((n,)),
        ],
        compiler_params=pltpu.CompilerParams(
            collective_id=5, has_side_effects=True, vmem_limit_bytes=32 * 1024 * 1024
        ),
        cost_estimate=pl.CostEstimate(flops=60000000, bytes_accessed=40000000, transcendentals=0),
        name="closing",
    )(part, resid, grads, small)


def attend(operands):
    queries, key_rows, values = operands
    scores = jnp.einsum(
        "qhe,khe->hqk", queries, key_rows, preferred_element_type=jnp.float32
    ) * HD ** (-0.5)
    row_max = jnp.max(scores, axis=-1, keepdims=True)
    shifted = jnp.exp(scores - row_max)
    row_total = jnp.sum(shifted, axis=-1, keepdims=True)
    probs = (shifted / row_total).astype(jnp.bfloat16)
    attended = jnp.einsum("hqk,khe->qhe", probs, values, preferred_element_type=jnp.float32).astype(
        jnp.bfloat16
    )
    return (attended, row_max + jnp.log(row_total))


def attend_back(operands):
    queries, key_rows, values, log_total, grad_attended = operands
    scores = jnp.einsum(
        "qhe,khe->hqk", queries, key_rows, preferred_element_type=jnp.float32
    ) * HD ** (-0.5)
    probs = jnp.exp(scores - log_total)
    grad_probs = jnp.einsum(
        "qhe,khe->hqk", grad_attended, values, preferred_element_type=jnp.float32
    )
    grad_values = jnp.einsum(
        "hqk,qhe->khe",
        probs.astype(jnp.bfloat16),
        grad_attended,
        preferred_element_type=jnp.float32,
    ).astype(jnp.bfloat16)
    row_dot = jnp.sum(probs * grad_probs, axis=-1, keepdims=True)
    grad_scores = (probs * (grad_probs - row_dot)).astype(jnp.bfloat16)
    grad_queries = (
        jnp.einsum("hqk,khe->qhe", grad_scores, key_rows, preferred_element_type=jnp.float32)
        * HD ** (-0.5)
    ).astype(jnp.bfloat16)
    grad_keys = (
        jnp.einsum("hqk,qhe->khe", grad_scores, queries, preferred_element_type=jnp.float32)
        * HD ** (-0.5)
    ).astype(jnp.bfloat16)
    return (grad_queries, grad_keys, grad_values)


def body(
    layer_input,
    qkv_weight,
    query_bias,
    value_bias,
    out_weight,
    out_bias,
    attn_norm_gain,
    attn_norm_bias,
    ffn_in_weight,
    ffn_in_bias,
    ffn_out_weight,
    ffn_out_bias,
    ffn_norm_gain,
    ffn_norm_bias,
    grad_output,
):
    tensor_parts = lax.axis_size("tensor")
    tensor_rank = lax.axis_index("tensor")
    heads_here = HEADS // tensor_parts
    width_here = heads_here * HD
    hidden_here = FF // tensor_parts
    dp_parts = lax.axis_size("dp")
    ffn_in_full, ffn_out_full = (
        lax.all_gather(ffn_in_weight, "dp", axis=0, tiled=True),
        lax.all_gather(ffn_out_weight, "dp", axis=1, tiled=True),
    )
    seq_count, piece_len, feature_count = layer_input.shape
    length = piece_len * tensor_parts
    row_count = seq_count * length
    local_rows = seq_count * piece_len

    def by_piece(rows):
        rows = rows.astype(jnp.bfloat16).reshape(seq_count, tensor_parts, piece_len, feature_count)
        return rows.swapaxes(0, 1).reshape(tensor_parts, local_rows, feature_count)

    def by_row(pieces):
        pieces = pieces.reshape(tensor_parts, seq_count, piece_len, feature_count)
        return pieces.swapaxes(0, 1).reshape(row_count, feature_count)

    local_input = layer_input.reshape(local_rows, feature_count)
    input_pieces, qkv_slots, out_slots = opening(
        tensor_parts, dp_parts, local_input, qkv_weight, out_weight
    )
    input_rows = by_row(input_pieces)
    qkv_full = qkv_slots.reshape(feature_count, 3 * width_here)
    out_full = out_slots.swapaxes(0, 1).reshape(width_here, feature_count)
    packed = matmul(input_rows, qkv_full).reshape(seq_count, length, heads_here, 3, HD)
    query_slice = lax.dynamic_slice_in_dim(
        query_bias.reshape(HEADS, HD), tensor_rank * heads_here, heads_here, 0
    )
    value_slice = lax.dynamic_slice_in_dim(
        value_bias.reshape(HEADS, HD), tensor_rank * heads_here, heads_here, 0
    )
    queries = (packed[:, :, :, 0] + query_slice).astype(jnp.bfloat16)
    key_rows = packed[:, :, :, 1].astype(jnp.bfloat16)
    values = (packed[:, :, :, 2] + value_slice).astype(jnp.bfloat16)
    attended, log_total = lax.map(attend, (queries, key_rows, values))
    attended_rows = attended.reshape(row_count, width_here)
    wide = jax.ShapeDtypeStruct((local_rows, feature_count), jnp.float32)
    low = jax.ShapeDtypeStruct((local_rows, feature_count), jnp.bfloat16)
    sums = jax.ShapeDtypeStruct((3, feature_count), jnp.float32)
    normed_pieces, unit_one, inv_std_one, normed_low = turn(
        tensor_parts,
        1,
        "turn_one",
        middle_one,
        by_piece(matmul(attended_rows, out_full)),
        (local_input, out_bias[None], attn_norm_gain[None], attn_norm_bias[None]),
        [wide, jax.ShapeDtypeStruct((local_rows, 128), jnp.float32), low],
    )
    normed_rows = by_row(normed_pieces)
    inner_bias = lax.dynamic_slice_in_dim(ffn_in_bias, tensor_rank * hidden_here, hidden_here, 0)
    inner_pre = matmul(normed_rows, ffn_in_full) + inner_bias
    activated = gelu_exact(inner_pre).astype(jnp.bfloat16)
    branch_two_pieces, layer_output, grad_resid_two, small_two = turn(
        tensor_parts,
        2,
        "turn_two",
        middle_two,
        by_piece(matmul(activated, ffn_out_full)),
        (
            normed_low,
            ffn_out_bias[None],
            ffn_norm_gain[None],
            ffn_norm_bias[None],
            grad_output.reshape(local_rows, feature_count),
        ),
        [low, wide, sums],
    )
    layer_output = layer_output.reshape(layer_input.shape)
    grad_ffn_norm_gain, grad_ffn_norm_bias, grad_ffn_out_bias = small_two
    branch_two_rows = by_row(branch_two_pieces)
    grad_activated = matmul_by_transpose(branch_two_rows, ffn_out_full).astype(jnp.bfloat16)
    grad_ffn_out_local = transpose_matmul(activated, branch_two_rows)
    grad_inner = (grad_activated.astype(jnp.float32) * gelu_slope(inner_pre)).astype(jnp.bfloat16)
    inner_bias_grad = jnp.sum(grad_inner.astype(jnp.float32), axis=0)
    grad_ffn_in_local = transpose_matmul(normed_rows, grad_inner)
    shard_rows = feature_count // dp_parts
    normed_part = by_piece(matmul_by_transpose(grad_inner, ffn_in_full))
    ffn_in_local, ffn_out_local, normed_part = lax.optimization_barrier(
        (grad_ffn_in_local.astype(jnp.bfloat16), grad_ffn_out_local.astype(jnp.bfloat16), normed_part)
    )
    grad_ffn_in_weight = lax.psum_scatter(ffn_in_local, "dp", scatter_dimension=0, tiled=True).astype(jnp.float32)
    grad_ffn_out_weight = lax.psum_scatter(ffn_out_local, "dp", scatter_dimension=1, tiled=True).astype(jnp.float32)
    branch_one_pieces, grad_resid_one, small_one = turn(
        tensor_parts,
        3,
        "turn_three",
        middle_three,
        normed_part,
        (grad_resid_two, unit_one, inv_std_one, attn_norm_gain[None]),
        [wide, sums],
    )
    grad_attn_norm_gain, grad_attn_norm_bias, grad_out_bias = small_one
    branch_one_rows = by_row(branch_one_pieces)
    grad_attended = (
        matmul_by_transpose(branch_one_rows, out_full)
        .astype(jnp.bfloat16)
        .reshape(seq_count, length, heads_here, HD)
    )
    grad_out_local = transpose_matmul(branch_one_rows, attended_rows)
    grad_queries, grad_keys, grad_values = lax.map(
        attend_back, (queries, key_rows, values, log_total, grad_attended)
    )
    grad_packed = jnp.stack((grad_queries, grad_keys, grad_values), axis=3).reshape(
        row_count, 3 * width_here
    )
    grad_qkv_local = transpose_matmul(input_rows, grad_packed)
    query_grad_here = jnp.sum(grad_queries.astype(jnp.float32), axis=(0, 1)).reshape(width_here)
    value_grad_here = jnp.sum(grad_values.astype(jnp.float32), axis=(0, 1)).reshape(width_here)
    pieces = (
        query_grad_here,
        value_grad_here,
        inner_bias_grad,
        grad_out_bias,
        grad_attn_norm_gain,
        grad_attn_norm_bias,
        grad_ffn_out_bias,
        grad_ffn_norm_gain,
        grad_ffn_norm_bias,
    )
    small_size = sum(piece.shape[0] for piece in pieces)
    small = jnp.pad(jnp.concatenate(pieces), (0, -small_size % 1024)).reshape(-1, 128)
    attn_local = jnp.concatenate(
        (grad_qkv_local.astype(jnp.bfloat16), grad_out_local.astype(jnp.bfloat16)), axis=1
    ).reshape(dp_parts, shard_rows, 4 * width_here)
    grad_input, attn_grads, small_all = closing(
        tensor_parts,
        dp_parts,
        by_piece(matmul_by_transpose(grad_packed, qkv_full)),
        grad_resid_one,
        attn_local,
        small,
    )
    grad_input = grad_input.reshape(layer_input.shape)
    grad_qkv_weight = attn_grads[:, : 3 * width_here]
    grad_out_weight = attn_grads[:, 3 * width_here :].T
    flat = small_all.reshape(tensor_parts, -1)
    split = 2 * width_here + hidden_here
    common = jnp.sum(flat[:, split:small_size], axis=0).reshape(6, feature_count)
    summed = (
        flat[:, :width_here].reshape(-1),
        flat[:, width_here : 2 * width_here].reshape(-1),
        common[0],
        common[1],
        common[2],
        flat[:, 2 * width_here : split].reshape(-1),
        common[3],
        common[4],
        common[5],
    )
    return (
        layer_output,
        grad_input,
        grad_qkv_weight,
        summed[0],
        summed[1],
        grad_out_weight,
        summed[2],
        summed[3],
        summed[4],
        grad_ffn_in_weight,
        summed[5],
        grad_ffn_out_weight,
        summed[6],
        summed[7],
        summed[8],
    )


def solution(mesh):
    placed = (
        P("dp", "tensor", None),
        P("dp", "tensor"),
        P(),
        P(),
        P("tensor", "dp"),
        P(),
        P(),
        P(),
        P("dp", "tensor"),
        P(),
        P("tensor", "dp"),
        P(),
        P(),
        P(),
        P("dp", "tensor", None),
    )
    return jax.shard_map(
        body,
        mesh=mesh,
        in_specs=placed,
        out_specs=(
            P("dp", "tensor", None),
            P("dp", "tensor", None),
            P("dp", "tensor"),
            P(),
            P(),
            P("tensor", "dp"),
            P(),
            P(),
            P(),
            P("dp", "tensor"),
            P(),
            P("tensor", "dp"),
            P(),
            P(),
            P(),
        ),
        check_vma=False,
    )
```

```python
import functools

import jax
import jax.numpy as jnp
from jax import lax
from jax.experimental import pallas as pl
from jax.experimental.pallas import tpu as pltpu
from jax.sharding import PartitionSpec as P

HEADS = 16
HD = 64
FF = 4096


norm_eps = 1e-05
root_half = 0.7071067811865476
inv_root_tau = 0.3989422804014327


def matmul(first_op, second_op):
    return jnp.dot(first_op, second_op, preferred_element_type=jnp.float32)


def matmul_by_transpose(first_op, second_op):
    return lax.dot_general(
        first_op, second_op, (((1,), (1,)), ((), ())), preferred_element_type=jnp.float32
    )


def transpose_matmul(first_op, second_op):
    return lax.dot_general(
        first_op, second_op, (((0,), (0,)), ((), ())), preferred_element_type=jnp.float32
    )


def norm_forward(residual, norm_gain, offset):
    center = residual - jnp.mean(residual, axis=-1, keepdims=True)
    variance = jnp.mean(center * center, axis=-1, keepdims=True)
    inv_std = lax.rsqrt(variance + norm_eps)
    normed = center * inv_std
    return (normed * norm_gain + offset, normed, inv_std)


def norm_backward(upstream, normed, inv_std, norm_gain):
    scaled = upstream * norm_gain
    centered = scaled - jnp.mean(scaled, axis=-1, keepdims=True)
    return inv_std * (centered - normed * jnp.mean(scaled * normed, axis=-1, keepdims=True))


def gelu_exact(preact):
    return 0.5 * preact * (1.0 + lax.erf(preact * root_half))


def gelu_slope(preact):
    return (
        0.5 * (1.0 + lax.erf(preact * root_half))
        + preact * jnp.exp(-0.5 * preact * preact) * inv_root_tau
    )


MESH = pl.DeviceIdType.MESH
in_vmem = pl.BlockSpec(memory_space=pltpu.VMEM)
row_chunks = 2


def line_barrier(z, n):
    barrier = pltpu.get_barrier_semaphore()
    for there, other in ((z > 0, z - 1), (z < n - 1, z + 1)):

        @pl.when(there)
        def _():
            pl.semaphore_signal(barrier, inc=1, device_id={"tensor": other}, device_id_type=MESH)

    inner = (z > 0) & (z < n - 1)

    @pl.when(inner)
    def _():
        pl.semaphore_wait(barrier, 2)

    @pl.when(jnp.logical_not(inner))
    def _():
        pl.semaphore_wait(barrier, 1)


class LineSum:
    def __init__(self, z, n, part, stage, from_left, from_right, acc, send, recv):
        self.z, self.n = z, n
        self.part, self.stage, self.acc = part, stage, acc
        self.bufs, self.send, self.recv = (from_left, from_right), send, recv
        self.rows = part.shape[1] // row_chunks

    def at(self, c):
        return pl.ds(c * self.rows, self.rows)

    def copy(self, way, d, c, src):
        z, n = self.z, self.n
        other = lax.rem(z + 1, n) if way == 0 else lax.rem(z + n - 1, n)
        return pltpu.make_async_remote_copy(
            src_ref=src.at[d, self.at(c)],
            dst_ref=self.bufs[way].at[d, self.at(c)],
            send_sem=self.send.at[way, d, c],
            recv_sem=self.recv.at[way, d, c],
            device_id={"tensor": other},
            device_id_type=MESH,
        )

    def pairs(self):
        for k in range(self.n - 1):
            yield 0, self.n - 1 - k, self.z < self.n - 1 - k
            yield 1, k, self.z > k

    def start_ends(self):
        for c in range(row_chunks):
            for way, d, active in self.pairs():

                @pl.when(self.z == (0 if way == 0 else self.n - 1))
                def _():
                    self.copy(way, d, c, self.part).start()

    def forward(self, c):
        near_left = self.z < self.n // 2
        self.forward_way(0, c, near_left)
        self.forward_way(1, c, self.z >= 0)
        self.forward_way(0, c, jnp.logical_not(near_left))

    def forward_way(self, wanted, c, now):
        for way, d, active in self.pairs():
            if way != wanted:
                continue
            inner = self.z > 0 if way == 0 else self.z < self.n - 1

            @pl.when(active & inner & now)
            def _():
                self.copy(way, d, c, self.part).wait_recv()
                at = self.at(c)
                total = self.part[d, at].astype(jnp.float32) + self.bufs[way][d, at].astype(jnp.float32)
                self.stage[d, at] = total.astype(jnp.bfloat16)
                self.copy(way, d, c, self.stage).start()

    def finish(self, c):
        z, at = self.z, self.at(c)
        self.acc[at] = self.part[z, at].astype(jnp.float32)
        for way, there in ((0, z > 0), (1, z < self.n - 1)):

            @pl.when(there)
            def _():
                self.copy(way, z, c, self.part).wait_recv()
                self.acc[at] += self.bufs[way][z, at].astype(jnp.float32)

        return self.acc[at]

    def drain(self):
        for c in range(row_chunks):
            for way, d, active in self.pairs():

                @pl.when(active)
                def _():
                    self.copy(way, d, c, self.part).wait_send()


class LineGather:
    def __init__(self, z, n, full, send, recv):
        self.z, self.n, self.full, self.send, self.recv = z, n, full, send, recv
        self.rows = full.shape[1] // row_chunks

    def copy(self, way, s, c):
        z, n = self.z, self.n
        other = lax.rem(z + 1, n) if way == 0 else lax.rem(z + n - 1, n)
        block = self.full.at[s, pl.ds(c * self.rows, self.rows)]
        return pltpu.make_async_remote_copy(
            src_ref=block,
            dst_ref=block,
            send_sem=self.send.at[way, s, c],
            recv_sem=self.recv.at[s, c],
            device_id={"tensor": other},
            device_id_type=MESH,
        )

    def start(self, c):
        for way, there in ((0, self.z < self.n - 1), (1, self.z > 0)):

            @pl.when(there)
            def _():
                self.copy(way, self.z, c).start()

    def forward(self, c):
        for k in range(1, self.n):
            for way, s, there, onward in (
                (0, self.z - k, self.z >= k, self.z < self.n - 1),
                (1, self.z + k, self.z < self.n - k, self.z > 0),
            ):

                @pl.when(there)
                def _():
                    self.copy(way, s, c).wait_recv()

                    @pl.when(onward)
                    def _():
                        self.copy(way, s, c).start()

    def drain(self):
        for c in range(row_chunks):
            for s in range(self.n):
                for way, sent in (
                    (0, (self.z >= s) & (self.z < self.n - 1)),
                    (1, (self.z <= s) & (self.z > 0)),
                ):

                    @pl.when(sent)
                    def _():
                        self.copy(way, s, c).wait_send()


def turn_kernel(n, middle, side_count, out_count, *refs):
    part, side = refs[0], refs[1 : 1 + side_count]
    full, outs = refs[1 + side_count], refs[2 + side_count : 2 + side_count + out_count]
    stage, from_left, from_right, acc, sum_send, sum_recv, send, recv = refs[2 + side_count + out_count :]
    z = lax.axis_index("tensor")
    line_barrier(z, n)
    summing = LineSum(z, n, part, stage, from_left, from_right, acc, sum_send, sum_recv)
    gather = LineGather(z, n, full, send, recv)
    summing.start_ends()
    summing.forward(0)
    for c in range(row_chunks):
        if c + 1 < row_chunks:
            summing.forward(c + 1)
        total = summing.finish(c)
        full[z, summing.at(c)] = middle(c, summing.at(c), total, side, outs)
        gather.start(c)
        if c > 0:
            gather.forward(c - 1)
    gather.forward(row_chunks - 1)
    summing.drain()
    gather.drain()


def turn(n, number, name, middle, part, side, out_shapes):
    shape = part.shape
    return pl.pallas_call(
        functools.partial(turn_kernel, n, middle, len(side), len(out_shapes)),
        out_shape=[jax.ShapeDtypeStruct(shape, jnp.bfloat16)] + out_shapes,
        in_specs=[in_vmem] * (1 + len(side)),
        out_specs=[in_vmem] * (1 + len(out_shapes)),
        scratch_shapes=[pltpu.VMEM(shape, jnp.bfloat16)] * 3
        + [
            pltpu.VMEM(shape[1:], jnp.float32),
            pltpu.SemaphoreType.DMA((2, n, row_chunks)),
            pltpu.SemaphoreType.DMA((2, n, row_chunks)),
            pltpu.SemaphoreType.DMA((2, n, row_chunks)),
            pltpu.SemaphoreType.DMA((n, row_chunks)),
        ],
        compiler_params=pltpu.CompilerParams(
            collective_id=number, has_side_effects=True, vmem_limit_bytes=32 * 1024 * 1024
        ),
        cost_estimate=pl.CostEstimate(flops=60000000, bytes_accessed=40000000, transcendentals=0),
        name=name,
    )(part, *side)


def add_small(ref, c, values):
    for i, value in enumerate(values):
        row = jnp.sum(value, axis=0, keepdims=True)
        ref[i : i + 1] = row if c == 0 else ref[i : i + 1] + row


def middle_one(c, at, total, side, outs):
    layer_input, out_bias, gain, offset = side
    unit_out, inv_out, low_out = outs
    normed, unit, inv_std = norm_forward(
        layer_input[at].astype(jnp.float32) + (total + out_bias[...]), gain[...], offset[...]
    )
    low_value = normed.astype(jnp.bfloat16)
    unit_out[at] = unit
    inv_out[at] = jnp.broadcast_to(inv_std, (inv_std.shape[0], 128))
    low_out[at] = low_value
    return low_value


def middle_two(c, at, total, side, outs):
    low_in, bias, gain, offset, upstream = side
    output, resid_out, small = outs
    result, unit, inv_std = norm_forward(
        low_in[at].astype(jnp.float32) + (total + bias[...]), gain[...], offset[...]
    )
    output[at] = result.astype(jnp.bfloat16)
    grad_top = upstream[at].astype(jnp.float32)
    resid = norm_backward(grad_top, unit, inv_std, gain[...])
    resid_out[at] = resid
    branch = resid.astype(jnp.bfloat16)
    add_small(small, c, (grad_top * unit, grad_top, branch.astype(jnp.float32)))
    return branch


def middle_three(c, at, total, side, outs):
    resid_two, unit_one, inv_one, gain = side
    resid_out, small = outs
    grad_normed = total + resid_two[at]
    unit = unit_one[at]
    resid = norm_backward(grad_normed, unit, inv_one[at, 0:1], gain[...])
    resid_out[at] = resid
    branch = resid.astype(jnp.bfloat16)
    add_small(small, c, (grad_normed * unit, grad_normed, branch.astype(jnp.float32)))
    return branch


def place():
    p = lax.axis_index("dp")
    return p, lax.div(p, 2), lax.rem(p, 2), lax.axis_index("tensor")


def send_to(src, dst, send, recv, **peer):
    return pltpu.make_async_remote_copy(
        src_ref=src, dst_ref=dst, send_sem=send, recv_sem=recv, device_id=peer, device_id_type=MESH
    )


def greet_dp(barrier, groups, q, core):
    def signal(peer):
        pl.semaphore_signal(barrier, inc=1, device_id={"dp": peer}, device_id_type=MESH)

    signal(2 * q + 1 - core)

    def one(j, carry):
        signal(2 * lax.rem(q + j, groups) + core)
        return carry

    lax.fori_loop(1, groups, one, 0)


def opening_kernel(n, groups, x, first, second, x_full, first_full, second_full, *sems):
    p, q, core, z = place()
    send, recv, straight, pair, passed, from_peer, from_pair = sems
    weights = ((first, first_full), (second, second_full))
    barrier = pltpu.get_barrier_semaphore()
    greet_dp(barrier, groups, q, core)
    for there, other in ((z > 0, z - 1), (z < n - 1, z + 1)):

        @pl.when(there)
        def _():
            pl.semaphore_signal(barrier, inc=1, device_id={"tensor": other}, device_id_type=MESH)

    inner = (z > 0) & (z < n - 1)

    @pl.when(inner)
    def _():
        pl.semaphore_wait(barrier, groups + 2)

    @pl.when(jnp.logical_not(inner))
    def _():
        pl.semaphore_wait(barrier, groups + 1)

    def to_peer(w, j):
        shard, full = weights[w]
        peer = 2 * lax.rem(q + j, groups) + core
        return send_to(shard, full.at[p], straight.at[w, j], from_peer.at[w, q], dp=peer)

    def came(w, other):
        shard, full = weights[w]
        return send_to(
            shard, full.at[2 * other + core], straight.at[w, 0], from_peer.at[w, other], dp=2 * q + 1 - core
        )

    def to_pair(w, other):
        full = weights[w][1]
        block = full.at[2 * other + core]
        return send_to(block, block, passed.at[w, other], from_pair.at[w, other], dp=2 * q + 1 - core)

    def own_to_pair(w):
        shard, full = weights[w]
        return send_to(shard, full.at[p], pair.at[w], from_pair.at[w, q], dp=2 * q + 1 - core)

    def pair_came(w, other):
        shard, full = weights[w]
        return send_to(
            shard, full.at[2 * other + 1 - core], pair.at[w], from_pair.at[w, other], dp=2 * q + 1 - core
        )

    gather = LineGather(z, n, x_full, send, recv)
    x_full[z] = x[...]
    for c in range(row_chunks):
        gather.start(c)
    for w in range(2):

        def push(j, carry):
            to_peer(w, j).start()
            return carry

        lax.fori_loop(1, groups, push, 0)
        own_to_pair(w).start()
    for w in range(2):
        shard, full = weights[w]
        full[p] = shard[...]
    for c in range(row_chunks):
        gather.forward(c)
    for w in range(2):

        def forward(j, carry):
            other = lax.rem(q + groups - j, groups)
            came(w, other).wait_recv()
            to_pair(w, other).start()
            return carry

        lax.fori_loop(1, groups, forward, 0)
    for w in range(2):

        def collect(other, carry):
            pair_came(w, other).wait_recv()
            return carry

        lax.fori_loop(0, groups, collect, 0)

        def drain(j, carry):
            to_peer(w, j).wait_send()
            to_pair(w, lax.rem(q + groups - j, groups)).wait_send()
            return carry

        lax.fori_loop(1, groups, drain, 0)
        own_to_pair(w).wait_send()
    gather.drain()


def opening(n, devices, x, first, second):
    groups = devices // 2
    dma = pltpu.SemaphoreType.DMA
    low = jnp.bfloat16
    return pl.pallas_call(
        functools.partial(opening_kernel, n, groups),
        out_shape=[
            jax.ShapeDtypeStruct((n,) + x.shape, low),
            jax.ShapeDtypeStruct((devices,) + first.shape, low),
            jax.ShapeDtypeStruct((devices,) + second.shape, low),
        ],
        in_specs=[in_vmem] * 3,
        out_specs=[in_vmem] * 3,
        scratch_shapes=[
            dma((2, n, row_chunks)),
            dma((n, row_chunks)),
            dma((2, groups)),
            dma((2,)),
            dma((2, groups)),
            dma((2, groups)),
            dma((2, groups)),
        ],
        compiler_params=pltpu.CompilerParams(
            collective_id=4, has_side_effects=True, vmem_limit_bytes=32 * 1024 * 1024
        ),
        cost_estimate=pl.CostEstimate(flops=60000000, bytes_accessed=40000000, transcendentals=0),
        name="opening",
    )(x, first, second)


def closing_kernel(n, groups, part, resid, grads, small, grad_input, total, small_all, *scratch):
    stage, from_left, from_right, acc, pair_buf, mine, peer_buf, small_pair, small_sum = scratch[:9]
    (
        sum_send, sum_recv, pair_send, pair_recv, peer_send, peer_recv,
        small_pair_send, small_pair_recv, small_send, small_recv, end_send, end_recv,
    ) = scratch[9:]
    p, q, core, z = place()
    barrier = pltpu.get_barrier_semaphore()
    greet_dp(barrier, groups, q, core)
    for k in range(1, n):
        pl.semaphore_signal(
            barrier, inc=1, device_id={"tensor": lax.rem(z + k, n)}, device_id_type=MESH
        )
    pl.semaphore_wait(barrier, groups + n - 1)
    sibling = 2 * q + 1 - core

    def to_pair(other):
        return send_to(
            grads.at[2 * other + 1 - core], pair_buf.at[other], pair_send.at[other], pair_recv.at[other], dp=sibling
        )

    def to_peer(other):
        return send_to(
            mine.at[other], peer_buf.at[q], peer_send.at[other], peer_recv.at[q], dp=2 * other + core
        )

    def from_peer(other):
        return send_to(
            mine.at[other], peer_buf.at[other], peer_send.at[other], peer_recv.at[other], dp=2 * other + core
        )

    def small_to_peer(other):
        return send_to(
            small_sum.at[q], small_sum.at[q], small_send.at[other], small_recv.at[q], dp=2 * other + core
        )

    def small_from_peer(other):
        return send_to(
            small_sum.at[other], small_sum.at[other], small_send.at[other], small_recv.at[other], dp=2 * other + core
        )

    def small_on(k):
        there = lax.rem(z + k, n)
        return send_to(small_all.at[z], small_all.at[z], end_send.at[k], end_recv.at[z], tensor=there)

    def small_came(k):
        there = lax.rem(z + k, n)
        return send_to(small_all.at[there], small_all.at[there], end_send.at[k], end_recv.at[there], tensor=there)

    def others(body):
        def one(j, carry):
            body(lax.rem(q + j, groups))
            return carry

        lax.fori_loop(1, groups, one, 0)

    small_pair_copy = send_to(small, small_pair, small_pair_send, small_pair_recv, dp=sibling)
    small_pair_copy.start()
    others(lambda other: to_pair(other).start())
    to_pair(q).start()
    line = LineSum(z, n, part, stage, from_left, from_right, acc, sum_send, sum_recv)
    line.start_ends()
    small_pair_copy.wait_recv()
    small_sum[q] = small[...] + small_pair[...]
    others(lambda other: small_to_peer(other).start())

    def pass_on(other):
        to_pair(other).wait_recv()
        pair_total = grads[2 * other + core].astype(jnp.float32) + pair_buf[other].astype(jnp.float32)
        mine[other] = pair_total.astype(jnp.bfloat16)
        to_peer(other).start()

    others(pass_on)
    line.forward(0)
    line.forward(1)
    others(lambda other: small_from_peer(other).wait_recv())
    plane = small_sum[0]
    for other in range(1, groups):
        plane = plane + small_sum[other]
    small_all[z] = plane
    for k in range(1, n):
        small_on(k).start()
    for c in range(row_chunks):
        if c + 2 < row_chunks:
            line.forward(c + 2)
        at = line.at(c)
        grad_input[at] = (line.finish(c) + resid[at]).astype(jnp.bfloat16)
    to_pair(q).wait_recv()
    total[...] = grads[p].astype(jnp.float32) + pair_buf[q].astype(jnp.float32)

    def add_peer(other):
        from_peer(other).wait_recv()
        total[...] += peer_buf[other].astype(jnp.float32)

    others(add_peer)
    for k in range(1, n):
        small_came(k).wait_recv()
    line.drain()
    small_pair_copy.wait_send()
    to_pair(q).wait_send()

    def drain(other):
        to_pair(other).wait_send()
        to_peer(other).wait_send()
        small_to_peer(other).wait_send()

    others(drain)
    for k in range(1, n):
        small_on(k).wait_send()


def closing(n, devices, part, resid, grads, small):
    groups = devices // 2
    dma = pltpu.SemaphoreType.DMA
    low, wide = jnp.bfloat16, jnp.float32
    slab = grads.shape[1:]
    return pl.pallas_call(
        functools.partial(closing_kernel, n, groups),
        out_shape=[
            jax.ShapeDtypeStruct(resid.shape, low),
            jax.ShapeDtypeStruct(slab, wide),
            jax.ShapeDtypeStruct((n,) + small.shape, wide),
        ],
        in_specs=[in_vmem] * 4,
        out_specs=[in_vmem] * 3,
        scratch_shapes=[pltpu.VMEM(part.shape, low)] * 3
        + [
            pltpu.VMEM(part.shape[1:], wide),
            pltpu.VMEM((groups,) + slab, low),
            pltpu.VMEM((groups,) + slab, low),
            pltpu.VMEM((groups,) + slab, low),
            pltpu.VMEM(small.shape, wide),
            pltpu.VMEM((groups,) + small.shape, wide),
            dma((2, n, row_chunks)),
            dma((2, n, row_chunks)),
            dma((groups,)),
            dma((groups,)),
            dma((groups,)),
            dma((groups,)),
            dma(()),
            dma(()),
            dma((groups,)),
            dma((groups,)),
            dma((n,)),
            dma((n,)),
        ],
        compiler_params=pltpu.CompilerParams(
            collective_id=5, has_side_effects=True, vmem_limit_bytes=32 * 1024 * 1024
        ),
        cost_estimate=pl.CostEstimate(flops=60000000, bytes_accessed=40000000, transcendentals=0),
        name="closing",
    )(part, resid, grads, small)


def attend(operands):
    queries, key_rows, values = operands
    scores = jnp.einsum(
        "qhe,khe->hqk", queries, key_rows, preferred_element_type=jnp.float32
    ) * HD ** (-0.5)
    row_max = jnp.max(scores, axis=-1, keepdims=True)
    shifted = jnp.exp(scores - row_max)
    row_total = jnp.sum(shifted, axis=-1, keepdims=True)
    probs = (shifted / row_total).astype(jnp.bfloat16)
    attended = jnp.einsum("hqk,khe->qhe", probs, values, preferred_element_type=jnp.float32).astype(
        jnp.bfloat16
    )
    return (attended, row_max + jnp.log(row_total))


def attend_back(operands):
    queries, key_rows, values, log_total, grad_attended = operands
    scores = jnp.einsum(
        "qhe,khe->hqk", queries, key_rows, preferred_element_type=jnp.float32
    ) * HD ** (-0.5)
    probs = jnp.exp(scores - log_total)
    grad_probs = jnp.einsum(
        "qhe,khe->hqk", grad_attended, values, preferred_element_type=jnp.float32
    )
    grad_values = jnp.einsum(
        "hqk,qhe->khe",
        probs.astype(jnp.bfloat16),
        grad_attended,
        preferred_element_type=jnp.float32,
    ).astype(jnp.bfloat16)
    row_dot = jnp.sum(probs * grad_probs, axis=-1, keepdims=True)
    grad_scores = (probs * (grad_probs - row_dot)).astype(jnp.bfloat16)
    grad_queries = (
        jnp.einsum("hqk,khe->qhe", grad_scores, key_rows, preferred_element_type=jnp.float32)
        * HD ** (-0.5)
    ).astype(jnp.bfloat16)
    grad_keys = (
        jnp.einsum("hqk,qhe->khe", grad_scores, queries, preferred_element_type=jnp.float32)
        * HD ** (-0.5)
    ).astype(jnp.bfloat16)
    return (grad_queries, grad_keys, grad_values)


def body(
    layer_input,
    qkv_weight,
    query_bias,
    value_bias,
    out_weight,
    out_bias,
    attn_norm_gain,
    attn_norm_bias,
    ffn_in_weight,
    ffn_in_bias,
    ffn_out_weight,
    ffn_out_bias,
    ffn_norm_gain,
    ffn_norm_bias,
    grad_output,
):
    tensor_parts = lax.axis_size("tensor")
    tensor_rank = lax.axis_index("tensor")
    heads_here = HEADS // tensor_parts
    width_here = heads_here * HD
    hidden_here = FF // tensor_parts
    dp_parts = lax.axis_size("dp")
    ffn_in_full, ffn_out_full = (
        lax.all_gather(ffn_in_weight, "dp", axis=0, tiled=True),
        lax.all_gather(ffn_out_weight, "dp", axis=1, tiled=True),
    )
    seq_count, piece_len, feature_count = layer_input.shape
    length = piece_len * tensor_parts
    row_count = seq_count * length
    local_rows = seq_count * piece_len

    def by_piece(rows):
        rows = rows.astype(jnp.bfloat16).reshape(seq_count, tensor_parts, piece_len, feature_count)
        return rows.swapaxes(0, 1).reshape(tensor_parts, local_rows, feature_count)

    def by_row(pieces):
        pieces = pieces.reshape(tensor_parts, seq_count, piece_len, feature_count)
        return pieces.swapaxes(0, 1).reshape(row_count, feature_count)

    local_input = layer_input.reshape(local_rows, feature_count)
    input_pieces, qkv_slots, out_slots = opening(
        tensor_parts, dp_parts, local_input, qkv_weight, out_weight
    )
    input_rows = by_row(input_pieces)
    qkv_full = qkv_slots.reshape(feature_count, 3 * width_here)
    out_full = out_slots.swapaxes(0, 1).reshape(width_here, feature_count)
    packed = matmul(input_rows, qkv_full).reshape(seq_count, length, heads_here, 3, HD)
    query_slice = lax.dynamic_slice_in_dim(
        query_bias.reshape(HEADS, HD), tensor_rank * heads_here, heads_here, 0
    )
    value_slice = lax.dynamic_slice_in_dim(
        value_bias.reshape(HEADS, HD), tensor_rank * heads_here, heads_here, 0
    )
    queries = (packed[:, :, :, 0] + query_slice).astype(jnp.bfloat16)
    key_rows = packed[:, :, :, 1].astype(jnp.bfloat16)
    values = (packed[:, :, :, 2] + value_slice).astype(jnp.bfloat16)
    attended, log_total = lax.map(attend, (queries, key_rows, values))
    attended_rows = attended.reshape(row_count, width_here)
    wide = jax.ShapeDtypeStruct((local_rows, feature_count), jnp.float32)
    low = jax.ShapeDtypeStruct((local_rows, feature_count), jnp.bfloat16)
    sums = jax.ShapeDtypeStruct((3, feature_count), jnp.float32)
    normed_pieces, unit_one, inv_std_one, normed_low = turn(
        tensor_parts,
        1,
        "turn_one",
        middle_one,
        by_piece(matmul(attended_rows, out_full)),
        (local_input, out_bias[None], attn_norm_gain[None], attn_norm_bias[None]),
        [wide, jax.ShapeDtypeStruct((local_rows, 128), jnp.float32), low],
    )
    normed_rows = by_row(normed_pieces)
    inner_bias = lax.dynamic_slice_in_dim(ffn_in_bias, tensor_rank * hidden_here, hidden_here, 0)
    inner_pre = matmul(normed_rows, ffn_in_full) + inner_bias
    activated = gelu_exact(inner_pre).astype(jnp.bfloat16)
    branch_two_pieces, layer_output, grad_resid_two, small_two = turn(
        tensor_parts,
        2,
        "turn_two",
        middle_two,
        by_piece(matmul(activated, ffn_out_full)),
        (
            normed_low,
            ffn_out_bias[None],
            ffn_norm_gain[None],
            ffn_norm_bias[None],
            grad_output.reshape(local_rows, feature_count),
        ),
        [low, wide, sums],
    )
    layer_output = layer_output.reshape(layer_input.shape)
    grad_ffn_norm_gain, grad_ffn_norm_bias, grad_ffn_out_bias = small_two
    branch_two_rows = by_row(branch_two_pieces)
    grad_ffn_out_local = transpose_matmul(activated, branch_two_rows)
    ffn_out_local, branch_two_rows = lax.optimization_barrier(
        (grad_ffn_out_local.astype(jnp.bfloat16), branch_two_rows)
    )
    grad_activated = matmul_by_transpose(branch_two_rows, ffn_out_full).astype(jnp.bfloat16)
    grad_inner = (grad_activated.astype(jnp.float32) * gelu_slope(inner_pre)).astype(jnp.bfloat16)
    inner_bias_grad = jnp.sum(grad_inner.astype(jnp.float32), axis=0)
    grad_ffn_in_local = transpose_matmul(normed_rows, grad_inner)
    shard_rows = feature_count // dp_parts
    normed_part = by_piece(matmul_by_transpose(grad_inner, ffn_in_full))
    ffn_in_local, normed_part = lax.optimization_barrier(
        (grad_ffn_in_local.astype(jnp.bfloat16), normed_part)
    )
    grad_ffn_in_weight = lax.psum_scatter(ffn_in_local, "dp", scatter_dimension=0, tiled=True).astype(jnp.float32)
    grad_ffn_out_weight = lax.psum_scatter(ffn_out_local, "dp", scatter_dimension=1, tiled=True).astype(jnp.float32)
    branch_one_pieces, grad_resid_one, small_one = turn(
        tensor_parts,
        3,
        "turn_three",
        middle_three,
        normed_part,
        (grad_resid_two, unit_one, inv_std_one, attn_norm_gain[None]),
        [wide, sums],
    )
    grad_attn_norm_gain, grad_attn_norm_bias, grad_out_bias = small_one
    branch_one_rows = by_row(branch_one_pieces)
    grad_attended = (
        matmul_by_transpose(branch_one_rows, out_full)
        .astype(jnp.bfloat16)
        .reshape(seq_count, length, heads_here, HD)
    )
    grad_out_local = transpose_matmul(branch_one_rows, attended_rows)
    grad_queries, grad_keys, grad_values = lax.map(
        attend_back, (queries, key_rows, values, log_total, grad_attended)
    )
    grad_packed = jnp.stack((grad_queries, grad_keys, grad_values), axis=3).reshape(
        row_count, 3 * width_here
    )
    grad_qkv_local = transpose_matmul(input_rows, grad_packed)
    query_grad_here = jnp.sum(grad_queries.astype(jnp.float32), axis=(0, 1)).reshape(width_here)
    value_grad_here = jnp.sum(grad_values.astype(jnp.float32), axis=(0, 1)).reshape(width_here)
    pieces = (
        query_grad_here,
        value_grad_here,
        inner_bias_grad,
        grad_out_bias,
        grad_attn_norm_gain,
        grad_attn_norm_bias,
        grad_ffn_out_bias,
        grad_ffn_norm_gain,
        grad_ffn_norm_bias,
    )
    small_size = sum(piece.shape[0] for piece in pieces)
    small = jnp.pad(jnp.concatenate(pieces), (0, -small_size % 1024)).reshape(-1, 128)
    attn_local = jnp.concatenate(
        (grad_qkv_local.astype(jnp.bfloat16), grad_out_local.astype(jnp.bfloat16)), axis=1
    ).reshape(dp_parts, shard_rows, 4 * width_here)
    grad_input, attn_grads, small_all = closing(
        tensor_parts,
        dp_parts,
        by_piece(matmul_by_transpose(grad_packed, qkv_full)),
        grad_resid_one,
        attn_local,
        small,
    )
    grad_input = grad_input.reshape(layer_input.shape)
    grad_qkv_weight = attn_grads[:, : 3 * width_here]
    grad_out_weight = attn_grads[:, 3 * width_here :].T
    flat = small_all.reshape(tensor_parts, -1)
    split = 2 * width_here + hidden_here
    common = jnp.sum(flat[:, split:small_size], axis=0).reshape(6, feature_count)
    summed = (
        flat[:, :width_here].reshape(-1),
        flat[:, width_here : 2 * width_here].reshape(-1),
        common[0],
        common[1],
        common[2],
        flat[:, 2 * width_here : split].reshape(-1),
        common[3],
        common[4],
        common[5],
    )
    return (
        layer_output,
        grad_input,
        grad_qkv_weight,
        summed[0],
        summed[1],
        grad_out_weight,
        summed[2],
        summed[3],
        summed[4],
        grad_ffn_in_weight,
        summed[5],
        grad_ffn_out_weight,
        summed[6],
        summed[7],
        summed[8],
    )


def solution(mesh):
    placed = (
        P("dp", "tensor", None),
        P("dp", "tensor"),
        P(),
        P(),
        P("tensor", "dp"),
        P(),
        P(),
        P(),
        P("dp", "tensor"),
        P(),
        P("tensor", "dp"),
        P(),
        P(),
        P(),
        P("dp", "tensor", None),
    )
    return jax.shard_map(
        body,
        mesh=mesh,
        in_specs=placed,
        out_specs=(
            P("dp", "tensor", None),
            P("dp", "tensor", None),
            P("dp", "tensor"),
            P(),
            P(),
            P("tensor", "dp"),
            P(),
            P(),
            P(),
            P("dp", "tensor"),
            P(),
            P("tensor", "dp"),
            P(),
            P(),
            P(),
        ),
        check_vma=False,
    )
```
